256 devices in a mesh: section: 16 (over z_hi, y, core), seq: 16 (over x, z_lo).
Axes of the slice: x: 4, y: 4, z: 8 (z_hi: 2, z_lo: 4; z = z_hi * 4 + z_lo), core: 2. Of those that a mesh axis runs over, the one named last changes fastest.
Arguments:
- tokens_in: bfloat16 [6144, 2560], P('seq'), may hold values from -6 to 6
- stale_values: bfloat16 [16, 6144, 2560], P('section', 'seq'), may hold values from -6 to 6
- mod_scale: float32 [16, 2560], P('section'), may hold values from -0.5 to 0.5
- mod_shift: float32 [16, 2560], P('section'), may hold values from -3 to 3
- query_gain: float32 [16, 2560], P('section'), may hold values from -2.5 to 2.5
- key_gain: float32 [16, 2560], P('section'), may hold values from -2.5 to 2.5
- branch_gain: float32 [16, 2560], P('section'), may hold values from 1 to 3
- tile_list: int32 [96, 18], P('seq'), may hold values from 0 to 95, as said below
- tile_count: int32 [96], P('seq'), may hold values from 1 to 18
- patch_order: int32 [16, 6], P('seq'), may hold values from 0 to 5, each once within a row
Outputs:
- layer_out: bfloat16 [16, 6144, 2560], P('section', 'seq')
The draws below stay inside these ranges and needn't reach their ends.
Inputs may be any that keep to these rules, and one draw needn't show every extreme that they name: The first tile_count[g] entries of tile_list[g] are distinct, begin with g itself, and name tiles whose frame, tile row and tile column each differ from g's by at most one; later entries are valid tile numbers that are not read. `patch_order`: each row is a permutation of the block's 6 patches.
All inputs are finite; a program needn't handle non-finite values.
Results may differ from the reference program's by a relative error of at most 0.015.
Values may be sent and summed in bfloat16 or wider, within the bound.
No kernel may reach another device: no remote copies, remote signals or barrier semaphores. Data moves between devices by JAX's collectives and lax.ppermute only.
A program may use at most 128 MiB of HBM per device.

```python
import math
import jax
import jax.numpy as jnp
import numpy as np
from jax import lax

HD = 128
HEADS = 20
TILE = 64
HT = 2
WT = 3
C = 2560
NPATCH = 6
TOK_DEV = 384
TOKENS = 6144
TILES = 96
KMAX = 18
N_SECTION = 16
N_SEQ = 16


def tile_tables(key):
    offsets = [(0, 0, 0)]
    for step_f in (-1, 0, 1):
        for step_h in (-1, 0, 1):
            for step_w in (-1, 0, 1):
                if (step_f, step_h, step_w) != (0, 0, 0):
                    offsets.append((step_f, step_h, step_w))
    table = np.array(offsets, dtype=np.int32)
    delta_f = jnp.asarray(table[:, 0])
    delta_h = jnp.asarray(table[:, 1])
    delta_w = jnp.asarray(table[:, 2])
    offset_ids = jnp.arange(27, dtype=jnp.int32)
    tiles = jnp.arange(TILES, dtype=jnp.int32)
    frame = tiles // NPATCH
    row = tiles % NPATCH // WT
    column = tiles % WT
    next_f = frame[:, None] + delta_f[None, :]
    next_h = row[:, None] + delta_h[None, :]
    next_w = column[:, None] + delta_w[None, :]
    valid = (next_f >= 0) & (next_f < N_SEQ) & (next_h >= 0) & (next_h < HT) & (next_w >= 0) & (next_w < WT)
    target = next_f * NPATCH + next_h * WT + next_w
    coin = jax.random.randint(jax.random.fold_in(key, 1), (TILES, 27), 0, 4)
    keep = valid & ((coin != 0) | (offset_ids[None, :] == 0))
    full_frame = jax.random.randint(jax.random.fold_in(key, 2), (), 1, N_SEQ - 1)
    full_row = jax.random.randint(jax.random.fold_in(key, 3), (), 0, HT)
    full_col = jax.random.randint(jax.random.fold_in(key, 4), (), 1, WT - 1)
    full_tile = full_frame * NPATCH + full_row * WT + full_col
    keep = jnp.where((tiles == full_tile)[:, None], valid, keep)
    lone_tile = (full_tile + 1 + jax.random.randint(jax.random.fold_in(key, 5), (), 0, TILES - 1)) % TILES
    keep = jnp.where((tiles == lone_tile)[:, None], (offset_ids == 0)[None, :], keep)
    order_score = jnp.where(keep, 0, 64) + offset_ids[None, :]
    order = jnp.argsort(order_score, axis=1, stable=True)[:, :KMAX]
    picked_target = jnp.take_along_axis(target, order, axis=1)
    picked_keep = jnp.take_along_axis(keep, order, axis=1)
    filler = jax.random.randint(jax.random.fold_in(key, 6), (TILES, KMAX), 0, TILES)
    picked = jnp.where(picked_keep, picked_target, filler)
    counts = jnp.sum(keep.astype(jnp.int32), axis=1)
    return (picked.astype(jnp.int32), counts.astype(jnp.int32))


def draw_tile_list(key, part):
    picked, counts = tile_tables(key)
    return picked


def draw_tile_count(key, part):
    picked, counts = tile_tables(key)
    return counts


def block_levels(own_key, extent, cuts, smallest, high):
    def one(dim, blocks):
        heights = jax.random.uniform(jax.random.fold_in(jax.random.fold_in(own_key, 6), dim), (blocks,), jnp.float32, smallest / len(cuts), high / len(cuts))
        return jnp.repeat(jnp.exp(heights), extent[dim] // blocks).reshape((-1,) + (1,) * (len(extent) - dim - 1))

    level = one(*cuts[0])
    for cut in cuts[1:]:
        level = level * one(*cut)
    return level


def centred(rng, dims, deviation, bound, cuts=(), held_as=jnp.bfloat16):
    drawn = jax.random.normal(rng, dims, jnp.float32) * deviation
    if len(cuts) > 0:
        drawn = block_levels(rng, dims, cuts, -0.22, 0.18) * drawn
    return jnp.clip(drawn, min=-bound, max=bound).astype(held_as)


def setup_inputs(seed: int = 0) -> dict:
    seeds = jax.random.split(jax.random.key(seed), 11)
    tokens_in = centred(seeds[0], (TOKENS, C), 1.0, 6.0, ((0, 16),))
    stale_values = centred(seeds[1], (N_SECTION, TOKENS, C), 1.0, 6.0, ((0, 16), (1, 16)))
    mod_scale = jnp.clip(jax.random.uniform(seeds[2], (N_SECTION, C), jnp.float32, -0.5, 0.5) * block_levels(seeds[2], (N_SECTION, C), ((0, 16),), -0.4, 0.0), -0.5, 0.5)
    mod_shift = centred(seeds[3], (N_SECTION, C), 0.5, 3.0, ((0, 16),), jnp.float32)
    query_gain = jnp.clip(jax.random.uniform(seeds[4], (N_SECTION, C), jnp.float32, -2.5, 2.5) * block_levels(seeds[4], (N_SECTION, C), ((0, 16),), -0.4, 0.0), -2.5, 2.5)
    key_gain = jnp.clip(jax.random.uniform(seeds[5], (N_SECTION, C), jnp.float32, -2.5, 2.5) * block_levels(seeds[5], (N_SECTION, C), ((0, 16),), -0.4, 0.0), -2.5, 2.5)
    branch_gain = jnp.clip(1.0 + 2.0 * jax.random.uniform(seeds[6], (N_SECTION, C), jnp.float32) ** block_levels(seeds[6], (N_SECTION, C), ((0, 16),), -0.2, 0.2), 1.0, 3.0)
    tile_list = draw_tile_list(jax.random.fold_in(seeds[10], 71), 0)
    tile_count = draw_tile_count(jax.random.fold_in(seeds[10], 71), 0)
    patch_order = jax.vmap(lambda own: jax.random.permutation(own, NPATCH))(jax.random.split(seeds[9], N_SEQ)).reshape((N_SEQ, NPATCH)).astype(jnp.int32)
    return {"tokens_in": tokens_in, "stale_values": stale_values, "mod_scale": mod_scale, "mod_shift": mod_shift, "query_gain": query_gain, "key_gain": key_gain, "branch_gain": branch_gain, "tile_list": tile_list, "tile_count": tile_count, "patch_order": patch_order}


def head_norm(matrix):
    shaped = matrix.reshape(matrix.shape[0], HEADS, HD)
    power = lax.optimization_barrier(jnp.mean(shaped * shaped, axis=-1, keepdims=True))
    return (shaped * lax.rsqrt(power + 1e-06)).reshape(matrix.shape)

def keys_from(value_rows, gain):
    return (head_norm(value_rows.astype(jnp.float32)) * gain).astype(jnp.bfloat16)

def neighbour_rows(rows):
    padded = jnp.pad(rows.astype(jnp.float32), ((TOK_DEV, TOK_DEV), (0, 0))).reshape(N_SEQ + 2, TOK_DEV, HEADS, HD)
    return jnp.concatenate([padded[:-2], padded[2:]], axis=1)

def reference(tokens_in, stale_values, mod_scale, mod_shift, query_gain, key_gain, branch_gain, tile_list, tile_count, patch_order):
    tile_ids_all = jnp.arange(TILES, dtype=jnp.int32)
    slot_live = jnp.arange(KMAX, dtype=jnp.int32)[None, :] < tile_count[:, None]
    listed = jnp.any((tile_list[:, :, None] == tile_ids_all[None, None, :]) & slot_live[:, :, None], axis=1)
    listed_pad = jnp.pad(listed, ((0, 0), (NPATCH, NPATCH)))
    block_ids = jnp.arange(N_SEQ, dtype=jnp.int32)
    window_cols = block_ids[:, None] * NPATCH + jnp.arange(3 * NPATCH, dtype=jnp.int32)[None, :]
    score_scale = 1.0 / math.sqrt(HD)
    section_input = tokens_in
    outputs = []
    for section_index in range(N_SECTION):
        stale_v = stale_values[section_index]
        stale_k = keys_from(stale_v, key_gain[section_index])
        side_k = neighbour_rows(stale_k)
        side_v = neighbour_rows(stale_v)
        key_buf = stale_k
        value_buf = stale_v
        result = jnp.zeros((TOKENS, C), jnp.bfloat16)
        for position in range(NPATCH):
            tile_ids = block_ids * NPATCH + patch_order[:, position].astype(jnp.int32)
            row_ids = (tile_ids[:, None] * TILE + jnp.arange(TILE, dtype=jnp.int32)[None, :]).reshape(-1)
            block_rows = section_input[row_ids]
            hidden = head_norm(block_rows.astype(jnp.float32)) * (1.0 + mod_scale[section_index]) + mod_shift[section_index]
            value_rows = hidden.astype(jnp.bfloat16)
            key_rows = keys_from(value_rows, key_gain[section_index])
            query = (head_norm(hidden) * query_gain[section_index]).astype(jnp.bfloat16)
            key_buf = key_buf.at[row_ids].set(key_rows)
            value_buf = value_buf.at[row_ids].set(value_rows)
            query_f = query.astype(jnp.float32).reshape(N_SEQ, TILE, HEADS, HD)
            window = jnp.take_along_axis(listed_pad[tile_ids], window_cols, axis=1)
            side_mask = jnp.concatenate([window[:, :NPATCH], window[:, 2 * NPATCH:]], axis=1)
            local_mask = window[:, NPATCH:2 * NPATCH]
            side_tok = jnp.repeat(side_mask, TILE, axis=1)
            local_tok = jnp.repeat(local_mask, TILE, axis=1)
            side_scores = jnp.einsum('pqhd,pkhd->phqk', query_f, side_k) * score_scale
            side_w = jnp.where(side_tok[:, None, None, :], jnp.exp(side_scores), 0.0)
            side_den = lax.optimization_barrier(jnp.sum(side_w, axis=-1))
            side_num = jnp.einsum('phqk,pkhd->pqhd', side_w.astype(jnp.bfloat16).astype(jnp.float32), side_v)
            near_k = key_buf.astype(jnp.float32).reshape(N_SEQ, TOK_DEV, HEADS, HD)
            near_v = value_buf.astype(jnp.float32).reshape(N_SEQ, TOK_DEV, HEADS, HD)
            near_scores = jnp.einsum('pqhd,pkhd->phqk', query_f, near_k) * score_scale
            near_w = jnp.where(local_tok[:, None, None, :], jnp.exp(near_scores), 0.0)
            near_den = lax.optimization_barrier(jnp.sum(near_w, axis=-1))
            near_num = jnp.einsum('phqk,pkhd->pqhd', near_w.astype(jnp.bfloat16).astype(jnp.float32), near_v)
            denominator = jnp.transpose(side_den + near_den, (0, 2, 1))[..., None]
            mixed = ((side_num + near_num) / denominator).reshape(N_SEQ * TILE, C)
            out_rows = (block_rows.astype(jnp.float32) + branch_gain[section_index] * mixed).astype(jnp.bfloat16)
            result = result.at[row_ids].set(out_rows)
        outputs.append(result)
        section_input = result
    return jnp.stack(outputs)
```

```python
import functools
import math

import jax
import jax.numpy as jnp
from jax import lax
from jax.experimental import pallas as pl
from jax.experimental.pallas import tpu as pltpu
from jax.sharding import PartitionSpec as P

HD = 128
TILE = 64
HT = 2
WT = 3
NPATCH = 6
ROWS = 384
HALF = 192
CHANNELS = 2560
GROUP = 8
LAYERS = 8
KEYS = 1536
COLKEYS = 512
OWN_ROWS = 960
MASKED = -16384.0
QUERY_SCALE = math.log2(math.e) / math.sqrt(HD)
EPS = 1e-06

ANY = pl.BlockSpec(memory_space=pl.ANY)
VMEM = pl.BlockSpec(memory_space=pltpu.VMEM)
SMEM = pl.BlockSpec(memory_space=pltpu.SMEM)

QUERY_ROWS = ((0, 256), (0, 384), (128, 384))


def column_order():
    return [(row, column) for column in range(WT) for row in range(HT)]


def first_heads_kernel(values, chunk):
    for h in range(GROUP):
        chunk[h] = values[0, :, h * HD : (h + 1) * HD]


def by_owner_kernel(values, owned):
    for d in range(GROUP):
        second, head, half = GROUP + d, 2 * GROUP + d // 2, (d % 2) * HALF
        owned[d, :ROWS] = values[0, :, d * HD : (d + 1) * HD]
        owned[d, ROWS : 2 * ROWS] = values[0, :, second * HD : (second + 1) * HD]
        owned[d, 2 * ROWS :] = values[0, half : half + HALF, head * HD : (head + 1) * HD]


def home_kernel(first_head, place, *refs):
    pieces, sems, out = refs[:GROUP], refs[-1], refs[-2]
    mine = place[1]
    copies = []
    for k in range(GROUP):
        start = pl.multiple_of((first_head + lax.bitwise_xor(mine, k)) * HD, HD)
        copies.append(
            pltpu.make_async_copy(pieces[k], out.at[0, :, pl.ds(start, HD)], sems.at[k])
        )
    for copy in copies:
        copy.start()
    for copy in copies:
        copy.wait()


def home_last_kernel(first_head, place, *refs):
    pieces, sems, out = refs[:GROUP], refs[-1], refs[-2]
    mine = place[1]
    for core in range(2):

        @pl.when(lax.rem(mine, 2) == core)
        def _():
            copies = []
            for k in range(core, GROUP, 2):
                head = first_head + lax.div(lax.bitwise_xor(mine, k), 2)
                start = pl.multiple_of(head * HD, HD)
                copies.append(
                    pltpu.make_async_copy(pieces[k], out.at[0, :, pl.ds(start, HD)], sems.at[k])
                )
            for copy in copies:
                copy.start()
            for copy in copies:
                copy.wait()


def row_scale(matrix):
    return lax.rsqrt(jnp.mean(matrix * matrix, axis=-1, keepdims=True) + EPS)


def attention_kernel(spec, place, active_ref, x_in, params, bias, *refs):
    halves, chunk, from_tokens, n_kv, n_prev, own_offset, lo_offset, hi_offset = spec
    kv_refs = refs[:n_kv]
    outs = refs[n_kv + n_prev : n_kv + n_prev + GROUP]
    x_out = refs[n_kv + n_prev + GROUP]
    (x_buf, kv_buf, out_buf, key_buf, value_buf, query_buf, kv_sems, x_sem, out_sems) = refs[
        n_kv + n_prev + GROUP + 1 :
    ]
    mine = place[1]

    @pl.when(active_ref[0] == 1)
    def _():
        if from_tokens:
            if halves:
                head = 2 * GROUP + lax.div(mine, 2)
            else:
                head = chunk * GROUP + mine
            source = x_in.at[:, pl.ds(pl.multiple_of(head * HD, HD), HD)]
        else:
            source = x_in
        x_copy = pltpu.make_async_copy(source, x_buf, x_sem)
        x_copy.start()

        def kv_copies(layer):
            copies = []
            if halves:
                for i, (ref, offset) in enumerate(zip(kv_refs, (own_offset, 0, 0, 0, 0, 0))):
                    copies.append(
                        pltpu.make_async_copy(
                            ref.at[layer, pl.ds(offset, HALF)],
                            kv_buf.at[layer, i // 2, pl.ds((i % 2) * HALF, HALF)],
                            kv_sems.at[layer, i],
                        )
                    )
            else:
                for i, (ref, offset) in enumerate(
                    zip(kv_refs, (own_offset, lo_offset, hi_offset))
                ):
                    copies.append(
                        pltpu.make_async_copy(
                            ref.at[layer, pl.ds(offset, ROWS)],
                            kv_buf.at[layer, i],
                            kv_sems.at[layer, i],
                        )
                    )
            return copies

        for layer in range(LAYERS):
            for copy in kv_copies(layer):
                copy.start()

        tile_of_row = lax.broadcasted_iota(jnp.int32, (KEYS, HD), 0) // TILE
        tile_of_lane = lax.broadcasted_iota(jnp.int32, (KEYS, HD), 1)
        key_buf[:, HD:] = jnp.where(tile_of_row == tile_of_lane, 1.0, 0.0).astype(jnp.bfloat16)
        value_buf[:, HD:] = jnp.ones((KEYS, HD), jnp.bfloat16)
        query_buf[:, HD:] = bias[...]

        x_copy.wait()
        if from_tokens:
            x0 = jnp.concatenate(
                [
                    x_buf[(row * WT + column) * TILE : (row * WT + column + 1) * TILE]
                    for row, column in column_order()
                ],
                axis=0,
            )
        else:
            x0 = x_buf[...]

        def layer_step(layer, x):
            for copy in kv_copies(layer):
                copy.wait()

            def gain(i):
                return params[layer, i : i + 1, chunk * HD : (chunk + 1) * HD]

            key_gain = gain(3)
            for column in range(WT):
                for slot, which in ((0, 1), (2, 2), (4, 0)):
                    for row in range(HT):
                        at = column * COLKEYS + (slot + row) * TILE
                        tile = (row * WT + column) * TILE
                        stale = kv_buf[layer, which, tile : tile + TILE]
                        value_buf[at : at + TILE, :HD] = stale
                        wide = stale.astype(jnp.float32)
                        key_buf[at : at + TILE, :HD] = (
                            wide * row_scale(wide) * key_gain
                        ).astype(jnp.bfloat16)

            hidden = x * row_scale(x) * (1.0 + gain(0)) + gain(1)
            new_values = hidden.astype(jnp.bfloat16)
            wide_values = new_values.astype(jnp.float32)
            new_keys = (wide_values * row_scale(wide_values) * key_gain).astype(jnp.bfloat16)
            query_buf[:, :HD] = (hidden * row_scale(hidden) * (gain(2) * QUERY_SCALE)).astype(
                jnp.bfloat16
            )
            for column in range(WT):
                at = column * COLKEYS + 6 * TILE
                rows = slice(column * 2 * TILE, (column + 1) * 2 * TILE)
                value_buf[at : at + 2 * TILE, :HD] = new_values[rows]
                key_buf[at : at + 2 * TILE, :HD] = new_keys[rows]

            sums = []
            for column in range(WT):
                keys = slice(column * COLKEYS, (column + 1) * COLKEYS)
                first, last = QUERY_ROWS[column]
                scores = lax.dot_general(
                    query_buf[first:last],
                    key_buf[keys],
                    (((1,), (1,)), ((), ())),
                    preferred_element_type=jnp.float32,
                )
                weights = jnp.exp2(scores).astype(jnp.bfloat16)
                sums.append(
                    jnp.dot(weights, value_buf[keys], preferred_element_type=jnp.float32)
                )
            total = [
                sums[0][:128] + sums[1][:128],
                sums[0][128:] + sums[1][128:256] + sums[2][:128],
                sums[1][256:] + sums[2][128:],
            ]
            mixed = jnp.concatenate([t[:, :HD] / t[:, HD:] for t in total], axis=0)
            out = (x + gain(4) * mixed).astype(jnp.bfloat16)
            for i, (row, column) in enumerate(column_order()):
                tile = (row * WT + column) * TILE
                out_buf[layer, tile : tile + TILE] = out[i * TILE : (i + 1) * TILE]

            return out.astype(jnp.float32)

        last = lax.fori_loop(0, LAYERS, layer_step, x0.astype(jnp.float32))
        x_buf[...] = last.astype(jnp.bfloat16)
        copies = [
            pltpu.make_async_copy(out_buf.at[lax.bitwise_xor(mine, k)], outs[k], out_sems.at[k])
            for k in range(GROUP)
        ]
        copies.append(pltpu.make_async_copy(x_buf, x_out, out_sems.at[GROUP]))
        for copy in copies:
            copy.start()
        for copy in copies:
            copy.wait()


def attention(
    place, active, x_in, params, bias, kv, previous, halves, chunk, from_tokens, own, lo, hi
):
    n_kv, n_prev = len(kv), len(previous)
    spec = (halves, chunk, from_tokens, n_kv, n_prev, own, lo, hi)
    piece = jax.ShapeDtypeStruct((ROWS, HD), jnp.bfloat16)
    pushes = 2 * 2 * 2 * 256 * 256 * 896 * LAYERS
    return pl.pallas_call(
        functools.partial(attention_kernel, spec),
        out_shape=[piece] * (GROUP + 1),
        in_specs=[SMEM, SMEM, ANY, VMEM, VMEM] + [ANY] * (n_kv + n_prev),
        out_specs=[ANY] * (GROUP + 1),
        scratch_shapes=[
            pltpu.VMEM((ROWS, HD), jnp.bfloat16),
            pltpu.VMEM((LAYERS, 3, ROWS, HD), jnp.bfloat16),
            pltpu.VMEM((LAYERS, ROWS, HD), jnp.bfloat16),
            pltpu.VMEM((KEYS, 2 * HD), jnp.bfloat16),
            pltpu.VMEM((KEYS, 2 * HD), jnp.bfloat16),
            pltpu.VMEM((ROWS, 2 * HD), jnp.bfloat16),
            pltpu.SemaphoreType.DMA((LAYERS, 6 if halves else 3)),
            pltpu.SemaphoreType.DMA,
            pltpu.SemaphoreType.DMA((GROUP + 1,)),
        ],
        input_output_aliases={5 + n_kv + i: i for i in range(n_prev)},
        compiler_params=pltpu.CompilerParams(vmem_limit_bytes=24 * 1024 * 1024),
        cost_estimate=pl.CostEstimate(
            flops=pushes, bytes_accessed=3 * 786432, transcendentals=896 * 512 * LAYERS
        ),
    )(place, active, x_in, params, bias, *kv, *previous)


def bias_table(tile_list, tile_count, plan, block_index):
    slot_live = jnp.arange(tile_list.shape[1])[None, :] < tile_count[:, None]
    window_ids = (block_index - 1) * NPATCH + jnp.arange(3 * NPATCH)
    window = jnp.any(
        (tile_list[:, :, None] == window_ids[None, None, :]) & slot_live[:, :, None], axis=1
    )
    patches = jnp.arange(NPATCH)
    position = jnp.sum(jnp.where(plan[None, :] == patches[:, None], patches[None, :], 0), axis=1)
    is_new = position[None, :] <= position[:, None]
    near = window[:, NPATCH : 2 * NPATCH]
    kinds = [window[:, :NPATCH], window[:, 2 * NPATCH :], near & ~is_new, near & is_new]
    listed = jnp.stack(kinds, axis=1).reshape(NPATCH, 4, HT, WT).transpose(0, 3, 1, 2)
    listed = listed.reshape(HT, WT, 4 * NPATCH).transpose(1, 0, 2).reshape(NPATCH, 4 * NPATCH)
    bias = jnp.where(listed, 0.0, MASKED).astype(jnp.bfloat16)
    bias = jnp.pad(bias, ((0, 0), (0, HD - 4 * NPATCH)))
    return jnp.repeat(bias, TILE, axis=0)


def on_device(
    tokens_in,
    stale_values,
    mod_scale,
    mod_shift,
    query_gain,
    key_gain,
    branch_gain,
    tile_list,
    tile_count,
    patch_order,
):
    n_section, n_seq = lax.axis_size("section"), lax.axis_size("seq")
    section = lax.axis_index("section")
    mine = lax.rem(section, GROUP)
    upper = lax.div(section, GROUP)
    core = lax.rem(section, 2)
    groups = [list(range(GROUP)), list(range(GROUP, 2 * GROUP))]
    forward = [(i, i + 1) for i in range(n_seq - 1)]
    backward = [(i + 1, i) for i in range(n_seq - 1)]
    place = jnp.stack([section, mine]).astype(jnp.int32)

    def exchange(array):
        return lax.all_to_all(array, "section", 0, 0, axis_index_groups=groups, tiled=True)

    chunk0 = pl.pallas_call(
        first_heads_kernel,
        out_shape=jax.ShapeDtypeStruct((GROUP, ROWS, HD), jnp.bfloat16),
        grid=(1,),
        in_specs=[pl.BlockSpec((1, ROWS, GROUP * HD), lambda i: (0, 0, 0))],
        out_specs=pl.BlockSpec((GROUP, ROWS, HD), lambda i: (0, 0, 0)),
    )(stale_values)
    low0 = lax.ppermute(chunk0, "seq", forward)
    high0 = lax.ppermute(chunk0, "seq", backward)

    later_values, gains, _ = lax.optimization_barrier(
        (stale_values, (mod_scale, mod_shift, query_gain, key_gain, branch_gain), chunk0)
    )
    owned = pl.pallas_call(
        by_owner_kernel,
        out_shape=jax.ShapeDtypeStruct((GROUP, OWN_ROWS, HD), jnp.bfloat16),
        in_specs=[VMEM],
        out_specs=VMEM,
    )(later_values)
    own = exchange(owned)
    own1 = own[:, ROWS : 2 * ROWS]
    low1 = lax.ppermute(own1, "seq", forward)
    high1 = lax.ppermute(own1, "seq", backward)
    own2 = own[:, 2 * ROWS :]

    def to_first_core(array, step, from_core):
        pairs = []
        for s in range(from_core, n_section, 2):
            for f in range(n_seq):
                if 0 <= f + step < n_seq:
                    pairs.append((s * n_seq + f, (s - from_core) * n_seq + f + step))
        return lax.ppermute(array, ("section", "seq"), pairs)

    own2_other = to_first_core(own2, 0, 1)
    low2 = [to_first_core(own2, 1, c) for c in range(2)]
    high2 = [to_first_core(own2, -1, c) for c in range(2)]

    vectors = jnp.concatenate(gains, axis=0).reshape(5, 20, HD)
    vectors = jnp.concatenate(
        [
            vectors[:, :GROUP],
            vectors[:, GROUP : 2 * GROUP],
            jnp.repeat(vectors[:, 2 * GROUP :], 2, axis=1),
        ],
        axis=-1,
    ).transpose(1, 0, 2)
    params = exchange(vectors)
    bias = bias_table(tile_list, tile_count, patch_order[0], lax.axis_index("seq"))

    sides0 = exchange(jnp.concatenate([low0, high0], axis=1))

    chunks = [
        (False, [own, sides0, sides0], (0, 0, ROWS)),
        (False, [own, low1, high1], (ROWS, 0, 0)),
        (True, [own, own2_other] + low2 + high2, (2 * ROWS, 0, 0)),
    ]
    out = None
    for chunk, (halves, kv, offsets) in enumerate(chunks):
        works = (core == 0) if halves else True
        step = 2 if halves else 1

        def run(stage, x_in, previous):
            active = jnp.logical_and(upper == stage, works).astype(jnp.int32).reshape(1)
            return attention(
                place, active, x_in, params, bias, kv, previous, halves, chunk, stage == 0, *offsets
            )

        *pieces, x_last = run(0, tokens_in, [])
        x_next = lax.ppermute(
            x_last, "section", [(i, i + GROUP) for i in range(0, GROUP, step)]
        )
        *pieces, _ = run(1, x_next, pieces)
        arrived = [pieces[0]]
        for k in range(1, GROUP):
            pairs = [
                (base + i, base + (i ^ k)) for base in (0, GROUP) for i in range(0, GROUP, step)
            ]
            arrived.append(lax.ppermute(pieces[k], "section", pairs))
        kernel = home_last_kernel if halves else home_kernel
        first_head = 2 * GROUP if halves else chunk * GROUP
        before = [] if out is None else [out]
        out = pl.pallas_call(
            functools.partial(kernel, first_head),
            out_shape=jax.ShapeDtypeStruct((1, ROWS, CHANNELS), jnp.bfloat16),
            in_specs=[SMEM] + [VMEM] * GROUP + [ANY] * len(before),
            out_specs=ANY,
            scratch_shapes=[pltpu.SemaphoreType.DMA((GROUP,))],
            input_output_aliases={1 + GROUP: 0} if before else {},
        )(place, *arrived, *before)
    return out


def solution(mesh):
    return jax.shard_map(
        on_device,
        mesh=mesh,
        in_specs=(
            P("seq", None),
            P("section", "seq", None),
            P("section", None),
            P("section", None),
            P("section", None),
            P("section", None),
            P("section", None),
            P("seq", None),
            P("seq"),
            P("seq", None),
        ),
        out_specs=P("section", "seq", None),
        check_vma=False,
    )
```

```python
import functools
import math

import jax
import jax.numpy as jnp
from jax import lax
from jax.experimental import pallas as pl
from jax.experimental.pallas import tpu as pltpu
from jax.sharding import PartitionSpec as P

HD = 128
TILE = 64
HT = 2
WT = 3
NPATCH = 6
ROWS = 384
HALF = 192
CHANNELS = 2560
GROUP = 8
LAYERS = 8
KEYS = 1536
COLKEYS = 512
MASKED = -16384.0
QUERY_SCALE = math.log2(math.e) / math.sqrt(HD)
EPS = 1e-06

ANY = pl.BlockSpec(memory_space=pl.ANY)
VMEM = pl.BlockSpec(memory_space=pltpu.VMEM)
SMEM = pl.BlockSpec(memory_space=pltpu.SMEM)
HBM = pl.BlockSpec(memory_space=pltpu.HBM)

SMALL = pl.CostEstimate(flops=0, bytes_accessed=1024, transcendentals=0)

QUERY_ROWS = ((0, 256), (0, 384), (128, 384))


def column_order():
    return [(row, column) for column in range(WT) for row in range(HT)]


def eight_heads_kernel(values, chunk):
    for d in range(GROUP):
        chunk[d] = values[0, :, d * HD : (d + 1) * HD]


def by_owner_kernel(values, _, owned):
    for d in range(GROUP):
        second, head, half = GROUP + d, 2 * GROUP + d // 2, (d % 2) * HALF
        owned[d, :ROWS] = values[0, :, d * HD : (d + 1) * HD]
        owned[d, ROWS : 2 * ROWS] = values[0, :, second * HD : (second + 1) * HD]
        owned[d, 2 * ROWS :] = values[0, half : half + HALF, head * HD : (head + 1) * HD]


def split_kernel(owned, low, high, vectors, second, last):
    second[...] = owned[:, ROWS : 2 * ROWS]
    last[...] = owned[:, 2 * ROWS :]


def join_kernel(low, high, _, joined):
    joined[:, :ROWS] = low[...]
    joined[:, ROWS:] = high[...]


def pass_kernel(*refs):
    pass


def home_kernel(parts, *refs):
    sems, out = refs[-1], refs[-2]
    copies = []
    for piece, row, first_head, step in parts:
        for i, d in enumerate(range(0, GROUP, step)):
            copies.append(
                pltpu.make_async_copy(
                    refs[piece].at[d, pl.ds(row, ROWS)],
                    out.at[0, :, pl.ds((first_head + i) * HD, HD)],
                    sems.at[len(copies)],
                )
            )
    for copy in copies:
        copy.start()
    for copy in copies:
        copy.wait()


def row_scale(matrix):
    return lax.rsqrt(jnp.mean(matrix * matrix, axis=-1, keepdims=True) + EPS)


def attention_kernel(spec, place, x_in, params, bias, *refs):
    heads, stage, n_kv, n_skip, first_row = spec
    n_heads = len(heads)
    kv_refs = refs[:n_kv]
    layers_out, x_out = refs[n_kv + n_skip : n_kv + n_skip + 2]
    scratch = refs[n_kv + n_skip + 2 :]
    x_buf, kv_buf, out_buf = scratch[:3]
    key_bufs = scratch[3 : 3 + n_heads]
    value_bufs = scratch[3 + n_heads : 3 + 2 * n_heads]
    query_bufs = scratch[3 + 2 * n_heads : 3 + 3 * n_heads]
    kv_sems, x_sems, out_sems = scratch[3 + 3 * n_heads :]
    mine, upper = place[1], place[2]

    def work(count):
        def x_copy(h):
            chunk = heads[h][0]
            if stage == 0:
                head = 2 * GROUP + lax.div(mine, 2) if chunk == 2 else chunk * GROUP + mine
                source = x_in.at[:, pl.ds(pl.multiple_of(head * HD, HD), HD)]
            else:
                source = x_in.at[h]
            return pltpu.make_async_copy(source, x_buf.at[h], x_sems.at[h])

        def kv_copies(layer, h):
            return [
                pltpu.make_async_copy(
                    kv_refs[ref].at[layer, pl.ds(at, rows)],
                    kv_buf.at[h, layer, kind, pl.ds(to, rows)],
                    kv_sems.at[h, layer, i],
                )
                for i, (ref, at, rows, kind, to) in enumerate(heads[h][1])
            ]

        def out_copy(layer, h):
            return pltpu.make_async_copy(
                out_buf.at[h, layer],
                layers_out.at[layer, pl.ds(first_row + h * ROWS, ROWS)],
                out_sems.at[h, layer],
            )

        for h in range(count):
            x_copy(h).start()
        for layer in range(LAYERS):
            for h in range(count):
                for copy in kv_copies(layer, h):
                    copy.start()

        tile_of_row = lax.broadcasted_iota(jnp.int32, (KEYS, HD), 0) // TILE
        tile_of_lane = lax.broadcasted_iota(jnp.int32, (KEYS, HD), 1)
        one_hot = jnp.where(tile_of_row == tile_of_lane, 1.0, 0.0).astype(jnp.bfloat16)
        for h in range(count):
            key_bufs[h][:, HD:] = one_hot
            value_bufs[h][:, HD:] = jnp.ones((KEYS, HD), jnp.bfloat16)
            query_bufs[h][:, HD:] = bias[...]

        first = []
        for h in range(count):
            x_copy(h).wait()
            if stage == 0:
                x = jnp.concatenate(
                    [
                        x_buf[h, (row * WT + column) * TILE : (row * WT + column + 1) * TILE]
                        for row, column in column_order()
                    ],
                    axis=0,
                )
            else:
                x = x_buf[h]
            first.append(x.astype(jnp.float32))

        def layer_step(layer, xs):
            def gain(h, i):
                chunk = heads[h][0]
                return params[layer, i : i + 1, chunk * HD : (chunk + 1) * HD]

            for h in range(count):
                for copy in kv_copies(layer, h):
                    copy.wait()
            for h in range(count):
                key_gain = gain(h, 3)
                for column in range(WT):
                    for slot, which in ((0, 1), (2, 2), (4, 0)):
                        for row in range(HT):
                            at = column * COLKEYS + (slot + row) * TILE
                            tile = (row * WT + column) * TILE
                            stale = kv_buf[h, layer, which, tile : tile + TILE]
                            value_bufs[h][at : at + TILE, :HD] = stale
                            wide = stale.astype(jnp.float32)
                            key_bufs[h][at : at + TILE, :HD] = (
                                wide * row_scale(wide) * key_gain
                            ).astype(jnp.bfloat16)

            for h in range(count):
                x = xs[h]
                hidden = x * row_scale(x) * (1.0 + gain(h, 0)) + gain(h, 1)
                new_values = hidden.astype(jnp.bfloat16)
                scaled = hidden * row_scale(hidden)
                new_keys = (scaled * gain(h, 3)).astype(jnp.bfloat16)
                query_bufs[h][:, :HD] = (scaled * (gain(h, 2) * QUERY_SCALE)).astype(jnp.bfloat16)
                for column in range(WT):
                    at = column * COLKEYS + 6 * TILE
                    rows = slice(column * 2 * TILE, (column + 1) * 2 * TILE)
                    value_bufs[h][at : at + 2 * TILE, :HD] = new_values[rows]
                    key_bufs[h][at : at + 2 * TILE, :HD] = new_keys[rows]

            sums = [[] for _ in range(count)]
            for column in range(WT):
                keys = slice(column * COLKEYS, (column + 1) * COLKEYS)
                begin, end = QUERY_ROWS[column]
                for h in range(count):
                    scores = lax.dot_general(
                        query_bufs[h][begin:end],
                        key_bufs[h][keys],
                        (((1,), (1,)), ((), ())),
                        preferred_element_type=jnp.float32,
                    )
                    weights = jnp.exp2(scores).astype(jnp.bfloat16)
                    sums[h].append(
                        jnp.dot(weights, value_bufs[h][keys], preferred_element_type=jnp.float32)
                    )
            results = []
            for h in range(count):
                left, middle, right = sums[h]
                total = [
                    left[:128] + middle[:128],
                    left[128:] + middle[128:256] + right[:128],
                    middle[256:] + right[128:],
                ]
                mixed = jnp.concatenate([t[:, :HD] / t[:, HD:] for t in total], axis=0)
                out = (xs[h] + gain(h, 4) * mixed).astype(jnp.bfloat16)
                for i, (row, column) in enumerate(column_order()):
                    tile = (row * WT + column) * TILE
                    out_buf[h, layer, tile : tile + TILE] = out[i * TILE : (i + 1) * TILE]
                out_copy(layer, h).start()
                results.append(out.astype(jnp.float32))
            return tuple(results)

        last = lax.fori_loop(0, LAYERS, layer_step, tuple(first))
        ends = []
        for h in range(count):
            x_buf[h] = last[h].astype(jnp.bfloat16)
            ends.append(pltpu.make_async_copy(x_buf.at[h], x_out.at[h], x_sems.at[h]))
            ends[-1].start()
        for h in range(count):
            for layer in range(LAYERS):
                out_copy(layer, h).wait()
            ends[h].wait()

    works = upper == stage
    if heads[0][0] == 2:
        works = works & (lax.rem(mine, 2) == 0)
    pl.when(works)(lambda: work(n_heads))


def attention(place, x_in, params, bias, kv, heads, stage, previous, before, first_row, rows):
    n_heads = len(heads)
    skipped = list(previous) + list(before)
    n_copies = max(len(head[1]) for head in heads)
    return pl.pallas_call(
        functools.partial(attention_kernel, (heads, stage, len(kv), len(skipped), first_row)),
        out_shape=[
            jax.ShapeDtypeStruct((LAYERS, rows, HD), jnp.bfloat16),
            jax.ShapeDtypeStruct((n_heads, ROWS, HD), jnp.bfloat16),
        ],
        in_specs=[SMEM, HBM if stage == 0 else ANY, VMEM, VMEM]
        + [ANY] * len(kv)
        + [HBM] * len(previous)
        + [ANY] * len(before),
        out_specs=[HBM, ANY],
        scratch_shapes=[
            pltpu.VMEM((n_heads, ROWS, HD), jnp.bfloat16),
            pltpu.VMEM((n_heads, LAYERS, 3, ROWS, HD), jnp.bfloat16),
            pltpu.VMEM((n_heads, LAYERS, ROWS, HD), jnp.bfloat16),
        ]
        + [pltpu.VMEM((KEYS, 2 * HD), jnp.bfloat16)] * (2 * n_heads)
        + [pltpu.VMEM((ROWS, 2 * HD), jnp.bfloat16)] * n_heads
        + [
            pltpu.SemaphoreType.DMA((n_heads, LAYERS, n_copies)),
            pltpu.SemaphoreType.DMA((n_heads,)),
            pltpu.SemaphoreType.DMA((n_heads, LAYERS)),
        ],
        input_output_aliases={4 + len(kv): 0} if previous else {},
        compiler_params=pltpu.CompilerParams(vmem_limit_bytes=32 * 1024 * 1024),
        cost_estimate=SMALL,
    )(place, x_in, params, bias, *kv, *skipped)


def bias_table(tile_list, tile_count, plan, block_index):
    slot_live = jnp.arange(tile_list.shape[1])[None, :] < tile_count[:, None]
    window_ids = (block_index - 1) * NPATCH + jnp.arange(3 * NPATCH)
    window = jnp.any(
        (tile_list[:, :, None] == window_ids[None, None, :]) & slot_live[:, :, None], axis=1
    )
    patches = jnp.arange(NPATCH)
    position = jnp.sum(jnp.where(plan[None, :] == patches[:, None], patches[None, :], 0), axis=1)
    is_new = position[None, :] <= position[:, None]
    near = window[:, NPATCH : 2 * NPATCH]
    kinds = [window[:, :NPATCH], window[:, 2 * NPATCH :], near & ~is_new, near & is_new]
    listed = jnp.stack(kinds, axis=1).reshape(NPATCH, 4, HT, WT).transpose(0, 3, 1, 2)
    listed = listed.reshape(HT, WT, 4 * NPATCH).transpose(1, 0, 2).reshape(NPATCH, 4 * NPATCH)
    bias = jnp.where(listed, 0.0, MASKED).astype(jnp.bfloat16)
    bias = jnp.pad(bias, ((0, 0), (0, HD - 4 * NPATCH)))
    return jnp.repeat(bias, TILE, axis=0)


def on_device(
    tokens_in,
    stale_values,
    mod_scale,
    mod_shift,
    query_gain,
    key_gain,
    branch_gain,
    tile_list,
    tile_count,
    patch_order,
):
    n_section, n_seq = lax.axis_size("section"), lax.axis_size("seq")
    section = lax.axis_index("section")
    mine = lax.rem(section, GROUP)
    upper = lax.div(section, GROUP)
    groups = [list(range(GROUP)), list(range(GROUP, 2 * GROUP))]
    forward = [(i, i + 1) for i in range(n_seq - 1)]
    backward = [(i + 1, i) for i in range(n_seq - 1)]
    place = jnp.stack([section, mine, upper]).astype(jnp.int32)

    def exchange(array):
        return lax.all_to_all(array, "section", 0, 0, axis_index_groups=groups, tiled=True)

    def both_ways(array):
        return lax.ppermute(array, "seq", forward), lax.ppermute(array, "seq", backward)

    def shape(*dims):
        return jax.ShapeDtypeStruct(dims, jnp.bfloat16)

    def call(kernel, out_shape, in_specs, out_specs, *args, **options):
        return pl.pallas_call(
            kernel,
            out_shape=out_shape,
            in_specs=in_specs,
            out_specs=out_specs,
            cost_estimate=SMALL,
            **options,
        )(*args)

    raw = call(
        eight_heads_kernel,
        shape(GROUP, ROWS, HD),
        [pl.BlockSpec((1, ROWS, GROUP * HD), lambda i: (0, 0, 0))],
        pl.BlockSpec((GROUP, ROWS, HD), lambda i: (0, 0, 0)),
        stale_values,
        grid=(1,),
    )
    raw_sides = both_ways(raw)
    own = exchange(
        call(
            by_owner_kernel,
            shape(GROUP, 2 * ROWS + HALF, HD),
            [VMEM, ANY],
            VMEM,
            stale_values,
            raw,
        )
    )

    vectors = jnp.concatenate(
        [mod_scale, mod_shift, query_gain, key_gain, branch_gain], axis=0
    ).reshape(5, 20, HD)
    vectors = jnp.concatenate(
        [
            vectors[:, :GROUP],
            vectors[:, GROUP : 2 * GROUP],
            jnp.repeat(vectors[:, 2 * GROUP :], 2, axis=1),
        ],
        axis=-1,
    ).transpose(1, 0, 2)
    vectors = call(
        pass_kernel,
        jax.ShapeDtypeStruct(vectors.shape, vectors.dtype),
        [HBM, ANY],
        HBM,
        vectors,
        own,
        input_output_aliases={0: 0},
    )
    params = exchange(vectors)
    bias = bias_table(tile_list, tile_count, patch_order[0], lax.axis_index("seq"))

    own_b, own_c = call(
        split_kernel,
        [shape(GROUP, ROWS, HD), shape(GROUP, HALF, HD)],
        [VMEM, ANY, ANY, ANY],
        [VMEM, VMEM],
        own,
        *raw_sides,
        params,
    )
    sides_b = both_ways(own_b)
    joined = call(
        join_kernel, shape(GROUP, 2 * ROWS, HD), [VMEM, VMEM, ANY], VMEM, *raw_sides, own_b
    )
    sides_a = exchange(joined)

    def to_first_core(array, step, from_core):
        pairs = []
        for s in range(from_core, n_section, 2):
            for f in range(n_seq):
                if 0 <= f + step < n_seq:
                    pairs.append((s * n_seq + f, (s - from_core) * n_seq + f + step))
        return lax.ppermute(array, ("section", "seq"), pairs)

    sides_c = [to_first_core(own_c, step, c) for step in (1, -1) for c in range(2)]
    own_c_other = to_first_core(own_c, 0, 1)

    head_a = (0, ((0, 0, ROWS, 0, 0), (1, 0, ROWS, 1, 0), (1, ROWS, ROWS, 2, 0)))
    head_b = (1, tuple((i, 0, ROWS, i, 0) for i in range(3)))
    head_c = (2, tuple((i, 0, HALF, i // 2, (i % 2) * HALF) for i in range(6)))
    kinds = {
        "a": ([own, sides_a], (head_a,), 0, 2 * ROWS),
        "b": ([own_b, *sides_b], (head_b,), ROWS, 2 * ROWS),
        "c": ([own_c, own_c_other, *sides_c], (head_c,), 0, ROWS),
    }

    def run(name, stage, x_in, previous, before):
        kv, heads, *rows = kinds[name]
        return attention(place, x_in, params, bias, kv, heads, stage, previous, before, *rows)

    def hop(last, step):
        return lax.ppermute(last, "section", [(i, i + GROUP) for i in range(0, GROUP, step)])

    def home(pieces, parts, out):
        before = [] if out is None else [out]
        return call(
            functools.partial(home_kernel, parts),
            shape(1, ROWS, CHANNELS),
            [VMEM] * len(pieces) + [HBM] * len(before),
            HBM,
            *pieces,
            *before,
            scratch_shapes=[pltpu.SemaphoreType.DMA((3 * GROUP,))],
            input_output_aliases={len(pieces): 0} if before else {},
        )

    layers, last_a = run("a", 0, tokens_in, [], [])
    next_a = hop(last_a, 1)
    layers, last_b = run("b", 0, tokens_in, [layers], [])
    next_b = hop(last_b, 1)
    layers, done_a = run("a", 1, next_a, [layers], [])
    layers_c, last_c = run("c", 0, tokens_in, [], [done_a, next_b])
    next_c = hop(last_c, 2)
    layers, done_b = run("b", 1, next_b, [layers], [last_c])
    layers = call(
        pass_kernel,
        shape(LAYERS, 2 * ROWS, HD),
        [HBM, ANY],
        HBM,
        layers,
        next_c,
        input_output_aliases={0: 0},
    )
    layers_c, _ = run("c", 1, next_c, [layers_c], [done_b])
    out = home([exchange(layers)], ((0, 0, 0, 1), (0, ROWS, GROUP, 1)), None)
    out = home([exchange(layers_c)], ((0, 0, 2 * GROUP, 2),), out)
    return out


def solution(mesh):
    return jax.shard_map(
        on_device,
        mesh=mesh,
        in_specs=(
            P("seq", None),
            P("section", "seq", None),
            P("section", None),
            P("section", None),
            P("section", None),
            P("section", None),
            P("section", None),
            P("seq", None),
            P("seq"),
            P("seq", None),
        ),
        out_specs=P("section", "seq", None),
        check_vma=False,
    )
```

```python
import functools
import math

import jax
import jax.numpy as jnp
from jax import lax
from jax.experimental import pallas as pl
from jax.experimental.pallas import tpu as pltpu
from jax.sharding import PartitionSpec as P

HD = 128
TILE = 64
HT = 2
WT = 3
NPATCH = 6
ROWS = 384
HALF = 192
CHANNELS = 2560
GROUP = 8
LAYERS = 8
KEYS = 1536
COLKEYS = 512
MASKED = -16384.0
QUERY_SCALE = math.log2(math.e) / math.sqrt(HD)
EPS = 1e-06

ANY = pl.BlockSpec(memory_space=pl.ANY)
VMEM = pl.BlockSpec(memory_space=pltpu.VMEM)
SMEM = pl.BlockSpec(memory_space=pltpu.SMEM)
HBM = pl.BlockSpec(memory_space=pltpu.HBM)

SMALL = pl.CostEstimate(flops=0, bytes_accessed=1024, transcendentals=0)

LARGE = pl.CostEstimate(flops=2**37, bytes_accessed=2**26, transcendentals=2**20)

QUERY_ROWS = ((0, 256), (0, 384), (128, 384))


def column_order():
    return [(row, column) for column in range(WT) for row in range(HT)]


def eight_heads_kernel(values, chunk):
    for d in range(GROUP):
        chunk[d] = values[0, :, d * HD : (d + 1) * HD]


def by_owner_kernel(values, _, owned):
    for d in range(GROUP):
        second, head, half = GROUP + d, 2 * GROUP + d // 2, (d % 2) * HALF
        owned[d, :ROWS] = values[0, :, d * HD : (d + 1) * HD]
        owned[d, ROWS : 2 * ROWS] = values[0, :, second * HD : (second + 1) * HD]
        owned[d, 2 * ROWS :] = values[0, half : half + HALF, head * HD : (head + 1) * HD]


def split_kernel(owned, low, high, vectors, second, last):
    second[...] = owned[:, ROWS : 2 * ROWS]
    last[...] = owned[:, 2 * ROWS :]


def join_kernel(low, high, _, joined):
    joined[:, :ROWS] = low[...]
    joined[:, ROWS:] = high[...]


def pass_kernel(*refs):
    pass


def home_kernel(parts, *refs):
    sems, out = refs[-1], refs[-2]
    copies = []
    for piece, row, first_head, step in parts:
        for i, d in enumerate(range(0, GROUP, step)):
            copies.append(
                pltpu.make_async_copy(
                    refs[piece].at[d, pl.ds(row, ROWS)],
                    out.at[0, :, pl.ds((first_head + i) * HD, HD)],
                    sems.at[len(copies)],
                )
            )
    for copy in copies:
        copy.start()
    for copy in copies:
        copy.wait()


def row_scale(matrix):
    return lax.rsqrt(jnp.mean(matrix * matrix, axis=-1, keepdims=True) + EPS)


def attention_kernel(spec, place, x_in, params, bias, *refs):
    heads, stage, n_kv, n_skip, first_row = spec
    n_heads = len(heads)
    kv_refs = refs[:n_kv]
    layers_out, x_out = refs[n_kv + n_skip : n_kv + n_skip + 2]
    scratch = refs[n_kv + n_skip + 2 :]
    x_buf, kv_buf, out_buf = scratch[:3]
    key_bufs = scratch[3 : 3 + n_heads]
    value_bufs = scratch[3 + n_heads : 3 + 2 * n_heads]
    query_bufs = scratch[3 + 2 * n_heads : 3 + 3 * n_heads]
    kv_sems, x_sems, out_sems = scratch[3 + 3 * n_heads :]
    mine, upper = place[1], place[2]

    def work(count):
        def x_copy(h):
            chunk = heads[h][0]
            if stage == 0:
                head = 2 * GROUP + lax.div(mine, 2) if chunk == 2 else chunk * GROUP + mine
                source = x_in.at[:, pl.ds(pl.multiple_of(head * HD, HD), HD)]
            else:
                source = x_in.at[h]
            return pltpu.make_async_copy(source, x_buf.at[h], x_sems.at[h])

        def kv_copies(layer, h):
            return [
                pltpu.make_async_copy(
                    kv_refs[ref].at[layer, pl.ds(at, rows)],
                    kv_buf.at[h, layer, kind, pl.ds(to, rows)],
                    kv_sems.at[h, layer, i],
                )
                for i, (ref, at, rows, kind, to) in enumerate(heads[h][1])
            ]

        def out_copy(layer, h):
            return pltpu.make_async_copy(
                out_buf.at[h, layer],
                layers_out.at[layer, pl.ds(first_row + h * ROWS, ROWS)],
                out_sems.at[h, layer],
            )

        for h in range(count):
            x_copy(h).start()
        for layer in range(LAYERS):
            for h in range(count):
                for copy in kv_copies(layer, h):
                    copy.start()

        tile_of_row = lax.broadcasted_iota(jnp.int32, (KEYS, HD), 0) // TILE
        tile_of_lane = lax.broadcasted_iota(jnp.int32, (KEYS, HD), 1)
        one_hot = jnp.where(tile_of_row == tile_of_lane, 1.0, 0.0).astype(jnp.bfloat16)
        for h in range(count):
            key_bufs[h][:, HD:] = one_hot
            value_bufs[h][:, HD:] = jnp.ones((KEYS, HD), jnp.bfloat16)
            query_bufs[h][:, HD:] = bias[...]

        first = []
        for h in range(count):
            x_copy(h).wait()
            if stage == 0:
                x = jnp.concatenate(
                    [
                        x_buf[h, (row * WT + column) * TILE : (row * WT + column + 1) * TILE]
                        for row, column in column_order()
                    ],
                    axis=0,
                )
            else:
                x = x_buf[h]
            first.append(x.astype(jnp.float32))

        def layer_step(layer, xs):
            def gain(h, i):
                chunk = heads[h][0]
                return params[layer, i : i + 1, chunk * HD : (chunk + 1) * HD]

            for h in range(count):
                for copy in kv_copies(layer, h):
                    copy.wait()
            for h in range(count):
                key_gain = gain(h, 3)
                for column in range(WT):
                    for slot, which in ((0, 1), (2, 2), (4, 0)):
                        for row in range(HT):
                            at = column * COLKEYS + (slot + row) * TILE
                            tile = (row * WT + column) * TILE
                            stale = kv_buf[h, layer, which, tile : tile + TILE]
                            value_bufs[h][at : at + TILE, :HD] = stale
                            wide = stale.astype(jnp.float32)
                            key_bufs[h][at : at + TILE, :HD] = (
                                wide * row_scale(wide) * key_gain
                            ).astype(jnp.bfloat16)

            for h in range(count):
                x = xs[h]
                hidden = x * row_scale(x) * (1.0 + gain(h, 0)) + gain(h, 1)
                new_values = hidden.astype(jnp.bfloat16)
                scaled = hidden * row_scale(hidden)
                new_keys = (scaled * gain(h, 3)).astype(jnp.bfloat16)
                query_bufs[h][:, :HD] = (scaled * (gain(h, 2) * QUERY_SCALE)).astype(jnp.bfloat16)
                for column in range(WT):
                    at = column * COLKEYS + 6 * TILE
                    rows = slice(column * 2 * TILE, (column + 1) * 2 * TILE)
                    value_bufs[h][at : at + 2 * TILE, :HD] = new_values[rows]
                    key_bufs[h][at : at + 2 * TILE, :HD] = new_keys[rows]

            sums = [[] for _ in range(count)]
            for column in range(WT):
                keys = slice(column * COLKEYS, (column + 1) * COLKEYS)
                begin, end = QUERY_ROWS[column]
                for h in range(count):
                    scores = lax.dot_general(
                        query_bufs[h][begin:end],
                        key_bufs[h][keys],
                        (((1,), (1,)), ((), ())),
                        preferred_element_type=jnp.float32,
                    )
                    weights = jnp.exp2(scores).astype(jnp.bfloat16)
                    sums[h].append(
                        jnp.dot(weights, value_bufs[h][keys], preferred_element_type=jnp.float32)
                    )
            results = []
            for h in range(count):
                left, middle, right = sums[h]
                total = [
                    left[:128] + middle[:128],
                    left[128:] + middle[128:256] + right[:128],
                    middle[256:] + right[128:],
                ]
                mixed = jnp.concatenate([t[:, :HD] / t[:, HD:] for t in total], axis=0)
                out = (xs[h] + gain(h, 4) * mixed).astype(jnp.bfloat16)
                for i, (row, column) in enumerate(column_order()):
                    tile = (row * WT + column) * TILE
                    out_buf[h, layer, tile : tile + TILE] = out[i * TILE : (i + 1) * TILE]
                out_copy(layer, h).start()
                results.append(out.astype(jnp.float32))
            return tuple(results)

        last = lax.fori_loop(0, LAYERS, layer_step, tuple(first))
        ends = []
        for h in range(count):
            x_buf[h] = last[h].astype(jnp.bfloat16)
            ends.append(pltpu.make_async_copy(x_buf.at[h], x_out.at[h], x_sems.at[h]))
            ends[-1].start()
        for h in range(count):
            for layer in range(LAYERS):
                out_copy(layer, h).wait()
            ends[h].wait()

    works = upper == stage
    if heads[0][0] == 2:
        works = works & (lax.rem(mine, 2) == 0)
    pl.when(works)(lambda: work(n_heads))


def attention(place, x_in, params, bias, kv, heads, stage, previous, before, first_row, rows, cost):
    n_heads = len(heads)
    skipped = list(previous) + list(before)
    n_copies = max(len(head[1]) for head in heads)
    return pl.pallas_call(
        functools.partial(attention_kernel, (heads, stage, len(kv), len(skipped), first_row)),
        out_shape=[
            jax.ShapeDtypeStruct((LAYERS, rows, HD), jnp.bfloat16),
            jax.ShapeDtypeStruct((n_heads, ROWS, HD), jnp.bfloat16),
        ],
        in_specs=[SMEM, HBM if stage == 0 else ANY, VMEM, VMEM]
        + [ANY] * len(kv)
        + [HBM] * len(previous)
        + [ANY] * len(before),
        out_specs=[HBM, ANY],
        scratch_shapes=[
            pltpu.VMEM((n_heads, ROWS, HD), jnp.bfloat16),
            pltpu.VMEM((n_heads, LAYERS, 3, ROWS, HD), jnp.bfloat16),
            pltpu.VMEM((n_heads, LAYERS, ROWS, HD), jnp.bfloat16),
        ]
        + [pltpu.VMEM((KEYS, 2 * HD), jnp.bfloat16)] * (2 * n_heads)
        + [pltpu.VMEM((ROWS, 2 * HD), jnp.bfloat16)] * n_heads
        + [
            pltpu.SemaphoreType.DMA((n_heads, LAYERS, n_copies)),
            pltpu.SemaphoreType.DMA((n_heads,)),
            pltpu.SemaphoreType.DMA((n_heads, LAYERS)),
        ],
        input_output_aliases={4 + len(kv): 0} if previous else {},
        compiler_params=pltpu.CompilerParams(vmem_limit_bytes=32 * 1024 * 1024),
        cost_estimate=cost,
    )(place, x_in, params, bias, *kv, *skipped)


def bias_table(tile_list, tile_count, plan, block_index):
    slot_live = jnp.arange(tile_list.shape[1])[None, :] < tile_count[:, None]
    window_ids = (block_index - 1) * NPATCH + jnp.arange(3 * NPATCH)
    window = jnp.any(
        (tile_list[:, :, None] == window_ids[None, None, :]) & slot_live[:, :, None], axis=1
    )
    patches = jnp.arange(NPATCH)
    position = jnp.sum(jnp.where(plan[None, :] == patches[:, None], patches[None, :], 0), axis=1)
    is_new = position[None, :] <= position[:, None]
    near = window[:, NPATCH : 2 * NPATCH]
    kinds = [window[:, :NPATCH], window[:, 2 * NPATCH :], near & ~is_new, near & is_new]
    listed = jnp.stack(kinds, axis=1).reshape(NPATCH, 4, HT, WT).transpose(0, 3, 1, 2)
    listed = listed.reshape(HT, WT, 4 * NPATCH).transpose(1, 0, 2).reshape(NPATCH, 4 * NPATCH)
    bias = jnp.where(listed, 0.0, MASKED).astype(jnp.bfloat16)
    bias = jnp.pad(bias, ((0, 0), (0, HD - 4 * NPATCH)))
    return jnp.repeat(bias, TILE, axis=0)


def on_device(
    tokens_in,
    stale_values,
    mod_scale,
    mod_shift,
    query_gain,
    key_gain,
    branch_gain,
    tile_list,
    tile_count,
    patch_order,
):
    n_section, n_seq = lax.axis_size("section"), lax.axis_size("seq")
    section = lax.axis_index("section")
    mine = lax.rem(section, GROUP)
    upper = lax.div(section, GROUP)
    groups = [list(range(GROUP)), list(range(GROUP, 2 * GROUP))]
    forward = [(i, i + 1) for i in range(n_seq - 1)]
    backward = [(i + 1, i) for i in range(n_seq - 1)]
    place = jnp.stack([section, mine, upper]).astype(jnp.int32)

    def exchange(array):
        return lax.all_to_all(array, "section", 0, 0, axis_index_groups=groups, tiled=True)

    def both_ways(array):
        return lax.ppermute(array, "seq", forward), lax.ppermute(array, "seq", backward)

    def shape(*dims):
        return jax.ShapeDtypeStruct(dims, jnp.bfloat16)

    def call(kernel, out_shape, in_specs, out_specs, *args, **options):
        return pl.pallas_call(
            kernel,
            out_shape=out_shape,
            in_specs=in_specs,
            out_specs=out_specs,
            cost_estimate=SMALL,
            **options,
        )(*args)

    raw = call(
        eight_heads_kernel,
        shape(GROUP, ROWS, HD),
        [pl.BlockSpec((1, ROWS, GROUP * HD), lambda i: (0, 0, 0))],
        pl.BlockSpec((GROUP, ROWS, HD), lambda i: (0, 0, 0)),
        stale_values,
        grid=(1,),
    )
    raw_sides = both_ways(raw)
    own = exchange(
        call(
            by_owner_kernel,
            shape(GROUP, 2 * ROWS + HALF, HD),
            [VMEM, ANY],
            VMEM,
            stale_values,
            raw,
        )
    )

    vectors = jnp.concatenate(
        [mod_scale, mod_shift, query_gain, key_gain, branch_gain], axis=0
    ).reshape(5, 20, HD)
    vectors = jnp.concatenate(
        [
            vectors[:, :GROUP],
            vectors[:, GROUP : 2 * GROUP],
            jnp.repeat(vectors[:, 2 * GROUP :], 2, axis=1),
        ],
        axis=-1,
    ).transpose(1, 0, 2)
    vectors = call(
        pass_kernel,
        jax.ShapeDtypeStruct(vectors.shape, vectors.dtype),
        [HBM, ANY],
        HBM,
        vectors,
        own,
        input_output_aliases={0: 0},
    )
    params = exchange(vectors)
    bias = bias_table(tile_list, tile_count, patch_order[0], lax.axis_index("seq"))

    own_b, own_c = call(
        split_kernel,
        [shape(GROUP, ROWS, HD), shape(GROUP, HALF, HD)],
        [VMEM, ANY, ANY, ANY],
        [VMEM, VMEM],
        own,
        *raw_sides,
        params,
    )
    sides_b = both_ways(own_b)
    joined = call(
        join_kernel, shape(GROUP, 2 * ROWS, HD), [VMEM, VMEM, ANY], VMEM, *raw_sides, own_b
    )
    sides_a = exchange(joined)

    def to_first_core(array, step, from_core):
        pairs = []
        for s in range(from_core, n_section, 2):
            for f in range(n_seq):
                if 0 <= f + step < n_seq:
                    pairs.append((s * n_seq + f, (s - from_core) * n_seq + f + step))
        return lax.ppermute(array, ("section", "seq"), pairs)

    sides_c = [to_first_core(own_c, step, c) for step in (1, -1) for c in range(2)]
    own_c_other = to_first_core(own_c, 0, 1)

    head_a = (0, ((0, 0, ROWS, 0, 0), (1, 0, ROWS, 1, 0), (1, ROWS, ROWS, 2, 0)))
    head_b = (1, tuple((i, 0, ROWS, i, 0) for i in range(3)))
    head_c = (2, tuple((i, 0, HALF, i // 2, (i % 2) * HALF) for i in range(6)))
    kinds = {
        "a": ([own, sides_a], (head_a,), 0, ROWS),
        "b": ([own_b, *sides_b], (head_b,), 0, 2 * ROWS),
        "c": ([own_c, own_c_other, *sides_c], (head_c,), ROWS, 2 * ROWS),
    }

    def run(name, stage, x_in, previous, before, cost=SMALL):
        kv, heads, *rows = kinds[name]
        return attention(place, x_in, params, bias, kv, heads, stage, previous, before, *rows, cost)

    def hop(last, step):
        return lax.ppermute(last, "section", [(i, i + GROUP) for i in range(0, GROUP, step)])

    def home(pieces, parts, out):
        before = [] if out is None else [out]
        return call(
            functools.partial(home_kernel, parts),
            shape(1, ROWS, CHANNELS),
            [VMEM] * len(pieces) + [HBM] * len(before),
            HBM,
            *pieces,
            *before,
            scratch_shapes=[pltpu.SemaphoreType.DMA((3 * GROUP,))],
            input_output_aliases={len(pieces): 0} if before else {},
        )

    layers_a, last_a = run("a", 0, tokens_in, [], [])
    next_a = hop(last_a, 1)
    layers, last_b = run("b", 0, tokens_in, [], [last_a])
    next_b = hop(last_b, 1)
    layers_a, done_a = run("a", 1, next_a, [layers_a], [last_b])
    arrived_a = exchange(layers_a)
    layers, last_c = run("c", 0, tokens_in, [layers], [done_a, next_b])
    next_c = hop(last_c, 2)
    layers, done_b = run("b", 1, next_b, [layers], [], LARGE)
    layers, _ = run("c", 1, next_c, [layers], [arrived_a])
    out = home([arrived_a], ((0, 0, 0, 1),), None)
    out = home([exchange(layers)], ((0, 0, GROUP, 1), (0, ROWS, 2 * GROUP, 2)), out)
    return out


def solution(mesh):
    return jax.shard_map(
        on_device,
        mesh=mesh,
        in_specs=(
            P("seq", None),
            P("section", "seq", None),
            P("section", None),
            P("section", None),
            P("section", None),
            P("section", None),
            P("section", None),
            P("seq", None),
            P("seq"),
            P("seq", None),
        ),
        out_specs=P("section", "seq", None),
        check_vma=False,
    )
```

```python
import functools
import math

import jax
import jax.numpy as jnp
from jax import lax
from jax.experimental import pallas as pl
from jax.experimental.pallas import tpu as pltpu
from jax.sharding import PartitionSpec as P

HD = 128
TILE = 64
HT = 2
WT = 3
NPATCH = 6
ROWS = 384
HALF = 192
CHANNELS = 2560
GROUP = 8
LAYERS = 8
KEYS = 1536
COLKEYS = 512
MASKED = -16384.0
QUERY_SCALE = math.log2(math.e) / math.sqrt(HD)
EPS = 1e-06

ANY = pl.BlockSpec(memory_space=pl.ANY)
VMEM = pl.BlockSpec(memory_space=pltpu.VMEM)
SMEM = pl.BlockSpec(memory_space=pltpu.SMEM)
HBM = pl.BlockSpec(memory_space=pltpu.HBM)

SMALL = pl.CostEstimate(flops=0, bytes_accessed=1024, transcendentals=0)

LARGE = pl.CostEstimate(flops=2**37, bytes_accessed=2**26, transcendentals=2**20)

QUERY_ROWS = ((0, 256), (0, 384), (128, 384))


def column_order():
    return [(row, column) for column in range(WT) for row in range(HT)]


def eight_heads_kernel(values, chunk):
    for d in range(GROUP):
        chunk[d] = values[0, :, d * HD : (d + 1) * HD]


def by_owner_kernel(values, _, owned):
    for d in range(GROUP):
        second, head, half = GROUP + d, 2 * GROUP + d // 2, (d % 2) * HALF
        owned[d, :ROWS] = values[0, :, d * HD : (d + 1) * HD]
        owned[d, ROWS : 2 * ROWS] = values[0, :, second * HD : (second + 1) * HD]
        owned[d, 2 * ROWS :] = values[0, half : half + HALF, head * HD : (head + 1) * HD]


def split_kernel(owned, low, high, vectors, second, last):
    second[...] = owned[:, ROWS : 2 * ROWS]
    last[...] = owned[:, 2 * ROWS :]


def join_kernel(low, high, _, joined):
    joined[:, :ROWS] = low[...]
    joined[:, ROWS:] = high[...]


def pass_kernel(*refs):
    pass


def home_kernel(parts, *refs):
    sems, out = refs[-1], refs[-2]
    copies = []
    for piece, row, first_head, step in parts:
        for i, d in enumerate(range(0, GROUP, step)):
            copies.append(
                pltpu.make_async_copy(
                    refs[piece].at[d, pl.ds(row, ROWS)],
                    out.at[0, :, pl.ds((first_head + i) * HD, HD)],
                    sems.at[len(copies)],
                )
            )
    for copy in copies:
        copy.start()
    for copy in copies:
        copy.wait()


def row_scale(matrix):
    return lax.rsqrt(jnp.mean(matrix * matrix, axis=-1, keepdims=True) + EPS)


def attention_kernel(spec, place, x_in, params, bias, *refs):
    heads, stage, n_kv, n_skip, first_row = spec
    n_heads = len(heads)
    kv_refs = refs[:n_kv]
    layers_out, x_out = refs[n_kv + n_skip : n_kv + n_skip + 2]
    scratch = refs[n_kv + n_skip + 2 :]
    x_buf, kv_buf, out_buf = scratch[:3]
    key_bufs = scratch[3 : 3 + n_heads]
    value_bufs = scratch[3 + n_heads : 3 + 2 * n_heads]
    query_bufs = scratch[3 + 2 * n_heads : 3 + 3 * n_heads]
    kv_sems, x_sems, out_sems = scratch[3 + 3 * n_heads :]
    mine, upper = place[1], place[2]

    def work(count):
        def x_copy(h):
            chunk = heads[h][0]
            if stage == 0:
                head = 2 * GROUP + lax.div(mine, 2) if chunk == 2 else chunk * GROUP + mine
                source = x_in.at[:, pl.ds(pl.multiple_of(head * HD, HD), HD)]
            else:
                source = x_in.at[h]
            return pltpu.make_async_copy(source, x_buf.at[h], x_sems.at[h])

        def kv_copies(layer, h):
            return [
                pltpu.make_async_copy(
                    kv_refs[ref].at[layer, pl.ds(at, rows)],
                    kv_buf.at[h, layer, kind, pl.ds(to, rows)],
                    kv_sems.at[h, layer, i],
                )
                for i, (ref, at, rows, kind, to) in enumerate(heads[h][1])
            ]

        def out_copy(layer, h):
            return pltpu.make_async_copy(
                out_buf.at[h, layer],
                layers_out.at[layer, pl.ds(first_row + h * ROWS, ROWS)],
                out_sems.at[h, layer],
            )

        for h in range(count):
            x_copy(h).start()
        for layer in range(LAYERS):
            for h in range(count):
                for copy in kv_copies(layer, h):
                    copy.start()

        tile_of_row = lax.broadcasted_iota(jnp.int32, (KEYS, HD), 0) // TILE
        tile_of_lane = lax.broadcasted_iota(jnp.int32, (KEYS, HD), 1)
        one_hot = jnp.where(tile_of_row == tile_of_lane, 1.0, 0.0).astype(jnp.bfloat16)
        for h in range(count):
            key_bufs[h][:, HD:] = one_hot
            value_bufs[h][:, HD:] = jnp.ones((KEYS, HD), jnp.bfloat16)
            query_bufs[h][:, HD:] = bias[...]

        first = []
        for h in range(count):
            x_copy(h).wait()
            if stage == 0:
                x = jnp.concatenate(
                    [
                        x_buf[h, (row * WT + column) * TILE : (row * WT + column + 1) * TILE]
                        for row, column in column_order()
                    ],
                    axis=0,
                )
            else:
                x = x_buf[h]
            first.append(x.astype(jnp.float32))

        def layer_step(layer, xs):
            def gain(h, i):
                chunk = heads[h][0]
                return params[layer, i : i + 1, chunk * HD : (chunk + 1) * HD]

            for h in range(count):
                for copy in kv_copies(layer, h):
                    copy.wait()
            for h in range(count):
                key_gain = gain(h, 3)
                for column in range(WT):
                    for slot, which in ((0, 1), (2, 2), (4, 0)):
                        for row in range(HT):
                            at = column * COLKEYS + (slot + row) * TILE
                            tile = (row * WT + column) * TILE
                            stale = kv_buf[h, layer, which, tile : tile + TILE]
                            value_bufs[h][at : at + TILE, :HD] = stale
                            wide = stale.astype(jnp.float32)
                            key_bufs[h][at : at + TILE, :HD] = (
                                wide * row_scale(wide) * key_gain
                            ).astype(jnp.bfloat16)

            for h in range(count):
                x = xs[h]
                hidden = x * row_scale(x) * (1.0 + gain(h, 0)) + gain(h, 1)
                new_values = hidden.astype(jnp.bfloat16)
                scaled = hidden * row_scale(hidden)
                new_keys = (scaled * gain(h, 3)).astype(jnp.bfloat16)
                query_bufs[h][:, :HD] = (scaled * (gain(h, 2) * QUERY_SCALE)).astype(jnp.bfloat16)
                for column in range(WT):
                    at = column * COLKEYS + 6 * TILE
                    rows = slice(column * 2 * TILE, (column + 1) * 2 * TILE)
                    value_bufs[h][at : at + 2 * TILE, :HD] = new_values[rows]
                    key_bufs[h][at : at + 2 * TILE, :HD] = new_keys[rows]

            sums = [[] for _ in range(count)]
            for column in range(WT):
                keys = slice(column * COLKEYS, (column + 1) * COLKEYS)
                begin, end = QUERY_ROWS[column]
                for h in range(count):
                    scores = lax.dot_general(
                        query_bufs[h][begin:end],
                        key_bufs[h][keys],
                        (((1,), (1,)), ((), ())),
                        preferred_element_type=jnp.float32,
                    )
                    weights = jnp.exp2(scores).astype(jnp.bfloat16)
                    sums[h].append(
                        jnp.dot(weights, value_bufs[h][keys], preferred_element_type=jnp.float32)
                    )
            results = []
            for h in range(count):
                left, middle, right = sums[h]
                total = [
                    left[:128] + middle[:128],
                    left[128:] + middle[128:256] + right[:128],
                    middle[256:] + right[128:],
                ]
                mixed = jnp.concatenate([t[:, :HD] / t[:, HD:] for t in total], axis=0)
                out = (xs[h] + gain(h, 4) * mixed).astype(jnp.bfloat16)
                for i, (row, column) in enumerate(column_order()):
                    tile = (row * WT + column) * TILE
                    out_buf[h, layer, tile : tile + TILE] = out[i * TILE : (i + 1) * TILE]
                out_copy(layer, h).start()
                results.append(out.astype(jnp.float32))
            return tuple(results)

        last = lax.fori_loop(0, LAYERS, layer_step, tuple(first))
        ends = []
        for h in range(count):
            x_buf[h] = last[h].astype(jnp.bfloat16)
            ends.append(pltpu.make_async_copy(x_buf.at[h], x_out.at[h], x_sems.at[h]))
            ends[-1].start()
        for h in range(count):
            for layer in range(LAYERS):
                out_copy(layer, h).wait()
            ends[h].wait()

    works = upper == stage
    if heads[0][0] == 2:
        works = works & (lax.rem(mine, 2) == 0)
    pl.when(works)(lambda: work(n_heads))


def attention(place, x_in, params, bias, kv, heads, stage, previous, before, first_row, rows, cost):
    n_heads = len(heads)
    skipped = list(previous) + list(before)
    n_copies = max(len(head[1]) for head in heads)
    return pl.pallas_call(
        functools.partial(attention_kernel, (heads, stage, len(kv), len(skipped), first_row)),
        out_shape=[
            jax.ShapeDtypeStruct((LAYERS, rows, HD), jnp.bfloat16),
            jax.ShapeDtypeStruct((n_heads, ROWS, HD), jnp.bfloat16),
        ],
        in_specs=[SMEM, HBM if stage == 0 else ANY, VMEM, VMEM]
        + [ANY] * len(kv)
        + [HBM] * len(previous)
        + [ANY] * len(before),
        out_specs=[HBM, ANY],
        scratch_shapes=[
            pltpu.VMEM((n_heads, ROWS, HD), jnp.bfloat16),
            pltpu.VMEM((n_heads, LAYERS, 3, ROWS, HD), jnp.bfloat16),
            pltpu.VMEM((n_heads, LAYERS, ROWS, HD), jnp.bfloat16),
        ]
        + [pltpu.VMEM((KEYS, 2 * HD), jnp.bfloat16)] * (2 * n_heads)
        + [pltpu.VMEM((ROWS, 2 * HD), jnp.bfloat16)] * n_heads
        + [
            pltpu.SemaphoreType.DMA((n_heads, LAYERS, n_copies)),
            pltpu.SemaphoreType.DMA((n_heads,)),
            pltpu.SemaphoreType.DMA((n_heads, LAYERS)),
        ],
        input_output_aliases={4 + len(kv): 0} if previous else {},
        compiler_params=pltpu.CompilerParams(vmem_limit_bytes=32 * 1024 * 1024),
        cost_estimate=cost,
    )(place, x_in, params, bias, *kv, *skipped)


def bias_table(tile_list, tile_count, plan, block_index):
    slot_live = jnp.arange(tile_list.shape[1])[None, :] < tile_count[:, None]
    window_ids = (block_index - 1) * NPATCH + jnp.arange(3 * NPATCH)
    window = jnp.any(
        (tile_list[:, :, None] == window_ids[None, None, :]) & slot_live[:, :, None], axis=1
    )
    patches = jnp.arange(NPATCH)
    position = jnp.sum(jnp.where(plan[None, :] == patches[:, None], patches[None, :], 0), axis=1)
    is_new = position[None, :] <= position[:, None]
    near = window[:, NPATCH : 2 * NPATCH]
    kinds = [window[:, :NPATCH], window[:, 2 * NPATCH :], near & ~is_new, near & is_new]
    listed = jnp.stack(kinds, axis=1).reshape(NPATCH, 4, HT, WT).transpose(0, 3, 1, 2)
    listed = listed.reshape(HT, WT, 4 * NPATCH).transpose(1, 0, 2).reshape(NPATCH, 4 * NPATCH)
    bias = jnp.where(listed, 0.0, MASKED).astype(jnp.bfloat16)
    bias = jnp.pad(bias, ((0, 0), (0, HD - 4 * NPATCH)))
    return jnp.repeat(bias, TILE, axis=0)


def on_device(
    tokens_in,
    stale_values,
    mod_scale,
    mod_shift,
    query_gain,
    key_gain,
    branch_gain,
    tile_list,
    tile_count,
    patch_order,
):
    n_section, n_seq = lax.axis_size("section"), lax.axis_size("seq")
    section = lax.axis_index("section")
    mine = lax.rem(section, GROUP)
    upper = lax.div(section, GROUP)
    groups = [list(range(GROUP)), list(range(GROUP, 2 * GROUP))]
    forward = [(i, i + 1) for i in range(n_seq - 1)]
    backward = [(i + 1, i) for i in range(n_seq - 1)]
    place = jnp.stack([section, mine, upper]).astype(jnp.int32)

    def exchange(array):
        return lax.all_to_all(array, "section", 0, 0, axis_index_groups=groups, tiled=True)

    def both_ways(array):
        return lax.ppermute(array, "seq", forward), lax.ppermute(array, "seq", backward)

    def shape(*dims):
        return jax.ShapeDtypeStruct(dims, jnp.bfloat16)

    def call(kernel, out_shape, in_specs, out_specs, *args, **options):
        return pl.pallas_call(
            kernel,
            out_shape=out_shape,
            in_specs=in_specs,
            out_specs=out_specs,
            cost_estimate=SMALL,
            **options,
        )(*args)

    raw = call(
        eight_heads_kernel,
        shape(GROUP, ROWS, HD),
        [pl.BlockSpec((1, ROWS, GROUP * HD), lambda i: (0, 0, 0))],
        pl.BlockSpec((GROUP, ROWS, HD), lambda i: (0, 0, 0)),
        stale_values,
        grid=(1,),
    )
    raw_sides = both_ways(raw)
    own = exchange(
        call(
            by_owner_kernel,
            shape(GROUP, 2 * ROWS + HALF, HD),
            [VMEM, ANY],
            VMEM,
            stale_values,
            raw,
        )
    )

    vectors = jnp.concatenate(
        [mod_scale, mod_shift, query_gain, key_gain, branch_gain], axis=0
    ).reshape(5, 20, HD)
    vectors = jnp.concatenate(
        [
            vectors[:, :GROUP],
            vectors[:, GROUP : 2 * GROUP],
            jnp.repeat(vectors[:, 2 * GROUP :], 2, axis=1),
        ],
        axis=-1,
    ).transpose(1, 0, 2)
    vectors = call(
        pass_kernel,
        jax.ShapeDtypeStruct(vectors.shape, vectors.dtype),
        [HBM, ANY],
        HBM,
        vectors,
        own,
        input_output_aliases={0: 0},
    )
    params = exchange(vectors)
    bias = bias_table(tile_list, tile_count, patch_order[0], lax.axis_index("seq"))

    own_b, own_c = call(
        split_kernel,
        [shape(GROUP, ROWS, HD), shape(GROUP, HALF, HD)],
        [VMEM, ANY, ANY, ANY],
        [VMEM, VMEM],
        own,
        *raw_sides,
        params,
    )
    sides_b = both_ways(own_b)
    joined = call(
        join_kernel, shape(GROUP, 2 * ROWS, HD), [VMEM, VMEM, ANY], VMEM, *raw_sides, own_b
    )
    sides_a = exchange(joined)

    def to_first_core(array, step, from_core):
        pairs = []
        for s in range(from_core, n_section, 2):
            for f in range(n_seq):
                if 0 <= f + step < n_seq:
                    pairs.append((s * n_seq + f, (s - from_core) * n_seq + f + step))
        return lax.ppermute(array, ("section", "seq"), pairs)

    sides_c = [to_first_core(own_c, step, c) for step in (1, -1) for c in range(2)]
    own_c_other = to_first_core(own_c, 0, 1)

    head_a = (0, ((0, 0, ROWS, 0, 0), (1, 0, ROWS, 1, 0), (1, ROWS, ROWS, 2, 0)))
    head_b = (1, tuple((i, 0, ROWS, i, 0) for i in range(3)))
    head_c = (2, tuple((i, 0, HALF, i // 2, (i % 2) * HALF) for i in range(6)))
    kinds = {
        "a": ([own, sides_a], (head_a,), 0, ROWS),
        "b": ([own_b, *sides_b], (head_b,), 0, 2 * ROWS),
        "c": ([own_c, own_c_other, *sides_c], (head_c,), ROWS, 2 * ROWS),
    }

    def run(name, stage, x_in, previous, before, cost=SMALL):
        kv, heads, *rows = kinds[name]
        return attention(place, x_in, params, bias, kv, heads, stage, previous, before, *rows, cost)

    def hop(last, step):
        return lax.ppermute(last, "section", [(i, i + GROUP) for i in range(0, GROUP, step)])

    def home(pieces, parts, out):
        before = [] if out is None else [out]
        return call(
            functools.partial(home_kernel, parts),
            shape(1, ROWS, CHANNELS),
            [VMEM] * len(pieces) + [HBM] * len(before),
            HBM,
            *pieces,
            *before,
            scratch_shapes=[pltpu.SemaphoreType.DMA((3 * GROUP,))],
            input_output_aliases={len(pieces): 0} if before else {},
        )

    layers_a, last_a = run("a", 0, tokens_in, [], [])
    next_a = hop(last_a, 1)
    layers, last_b = run("b", 0, tokens_in, [], [last_a], LARGE)
    next_b = hop(last_b, 1)
    layers_a, done_a = run("a", 1, next_a, [layers_a], [last_b])
    arrived_a = exchange(layers_a)
    layers, last_c = run("c", 0, tokens_in, [layers], [done_a, next_b])
    next_c = hop(last_c, 2)
    layers, done_b = run("b", 1, next_b, [layers], [], LARGE)
    layers, _ = run("c", 1, next_c, [layers], [arrived_a])
    out = home([arrived_a], ((0, 0, 0, 1),), None)
    out = home([exchange(layers)], ((0, 0, GROUP, 1), (0, ROWS, 2 * GROUP, 2)), out)
    return out


def solution(mesh):
    return jax.shard_map(
        on_device,
        mesh=mesh,
        in_specs=(
            P("seq", None),
            P("section", "seq", None),
            P("section", None),
            P("section", None),
            P("section", None),
            P("section", None),
            P("section", None),
            P("seq", None),
            P("seq"),
            P("seq", None),
        ),
        out_specs=P("section", "seq", None),
        check_vma=False,
    )
```

```python
import functools
import math

import jax
import jax.numpy as jnp
from jax import lax
from jax.experimental import pallas as pl
from jax.experimental.pallas import tpu as pltpu
from jax.sharding import PartitionSpec as P

HD = 128
TILE = 64
HT = 2
WT = 3
NPATCH = 6
ROWS = 384
HALF = 192
CHANNELS = 2560
GROUP = 8
LAYERS = 8
KEYS = 1536
COLKEYS = 512
MASKED = -16384.0
QUERY_SCALE = math.log2(math.e) / math.sqrt(HD)
EPS = 1e-06

ANY = pl.BlockSpec(memory_space=pl.ANY)
VMEM = pl.BlockSpec(memory_space=pltpu.VMEM)
SMEM = pl.BlockSpec(memory_space=pltpu.SMEM)
HBM = pl.BlockSpec(memory_space=pltpu.HBM)

SMALL = pl.CostEstimate(flops=0, bytes_accessed=1024, transcendentals=0)

LARGE = pl.CostEstimate(flops=2**37, bytes_accessed=2**26, transcendentals=2**20)

QUERY_ROWS = ((0, 256), (0, 384), (128, 384))


def column_order():
    return [(row, column) for column in range(WT) for row in range(HT)]


def eight_heads_kernel(values, chunk):
    for d in range(GROUP):
        chunk[d] = values[0, :, d * HD : (d + 1) * HD]


def by_owner_kernel(values, _, owned):
    for d in range(GROUP):
        second, head, half = GROUP + d, 2 * GROUP + d // 2, (d % 2) * HALF
        owned[d, :ROWS] = values[0, :, d * HD : (d + 1) * HD]
        owned[d, ROWS : 2 * ROWS] = values[0, :, second * HD : (second + 1) * HD]
        owned[d, 2 * ROWS :] = values[0, half : half + HALF, head * HD : (head + 1) * HD]


def split_kernel(owned, low, high, vectors, second, last):
    second[...] = owned[:, ROWS : 2 * ROWS]
    last[...] = owned[:, 2 * ROWS :]


def join_kernel(low, high, _, joined):
    joined[:, :ROWS] = low[...]
    joined[:, ROWS:] = high[...]


def pass_kernel(*refs):
    pass


def home_kernel(parts, *refs):
    sems, out = refs[-1], refs[-2]
    copies = []
    for piece, row, first_head, step in parts:
        for i, d in enumerate(range(0, GROUP, step)):
            copies.append(
                pltpu.make_async_copy(
                    refs[piece].at[d, pl.ds(row, ROWS)],
                    out.at[0, :, pl.ds((first_head + i) * HD, HD)],
                    sems.at[len(copies)],
                )
            )
    for copy in copies:
        copy.start()
    for copy in copies:
        copy.wait()


def row_scale(matrix):
    return lax.rsqrt(jnp.mean(matrix * matrix, axis=-1, keepdims=True) + EPS)


def attention_kernel(spec, place, x_in, params, bias, *refs):
    heads, stage, n_kv, n_skip, first_row = spec
    n_heads = len(heads)
    kv_refs = refs[:n_kv]
    layers_out, x_out = refs[n_kv + n_skip : n_kv + n_skip + 2]
    scratch = refs[n_kv + n_skip + 2 :]
    x_buf, kv_buf, out_buf = scratch[:3]
    key_bufs = scratch[3 : 3 + n_heads]
    value_bufs = scratch[3 + n_heads : 3 + 2 * n_heads]
    query_bufs = scratch[3 + 2 * n_heads : 3 + 3 * n_heads]
    kv_sems, x_sems, out_sems = scratch[3 + 3 * n_heads :]
    mine, upper = place[1], place[2]

    def work(count):
        def x_copy(h):
            chunk = heads[h][0]
            if stage == 0:
                head = 2 * GROUP + lax.div(mine, 2) if chunk == 2 else chunk * GROUP + mine
                source = x_in.at[:, pl.ds(pl.multiple_of(head * HD, HD), HD)]
            else:
                source = x_in.at[h]
            return pltpu.make_async_copy(source, x_buf.at[h], x_sems.at[h])

        def kv_copies(layer, h):
            return [
                pltpu.make_async_copy(
                    kv_refs[ref].at[layer, pl.ds(at, rows)],
                    kv_buf.at[h, layer, kind, pl.ds(to, rows)],
                    kv_sems.at[h, layer, i],
                )
                for i, (ref, at, rows, kind, to) in enumerate(heads[h][1])
            ]

        def out_copy(layer, h):
            return pltpu.make_async_copy(
                out_buf.at[h, layer],
                layers_out.at[layer, pl.ds(first_row + h * ROWS, ROWS)],
                out_sems.at[h, layer],
            )

        for h in range(count):
            x_copy(h).start()
        for layer in range(LAYERS):
            for h in range(count):
                for copy in kv_copies(layer, h):
                    copy.start()

        tile_of_row = lax.broadcasted_iota(jnp.int32, (KEYS, HD), 0) // TILE
        tile_of_lane = lax.broadcasted_iota(jnp.int32, (KEYS, HD), 1)
        one_hot = jnp.where(tile_of_row == tile_of_lane, 1.0, 0.0).astype(jnp.bfloat16)
        for h in range(count):
            key_bufs[h][:, HD:] = one_hot
            value_bufs[h][:, HD:] = jnp.ones((KEYS, HD), jnp.bfloat16)
            query_bufs[h][:, HD:] = bias[...]

        first = []
        for h in range(count):
            x_copy(h).wait()
            if stage == 0:
                x = jnp.concatenate(
                    [
                        x_buf[h, (row * WT + column) * TILE : (row * WT + column + 1) * TILE]
                        for row, column in column_order()
                    ],
                    axis=0,
                )
            else:
                x = x_buf[h]
            first.append(x.astype(jnp.float32))

        def layer_step(layer, xs):
            def gain(h, i):
                chunk = heads[h][0]
                return params[layer, i : i + 1, chunk * HD : (chunk + 1) * HD]

            for h in range(count):
                for copy in kv_copies(layer, h):
                    copy.wait()
            for h in range(count):
                key_gain = gain(h, 3)
                for column in range(WT):
                    for slot, which in ((0, 1), (2, 2), (4, 0)):
                        for row in range(HT):
                            at = column * COLKEYS + (slot + row) * TILE
                            tile = (row * WT + column) * TILE
                            stale = kv_buf[h, layer, which, tile : tile + TILE]
                            value_bufs[h][at : at + TILE, :HD] = stale
                            wide = stale.astype(jnp.float32)
                            key_bufs[h][at : at + TILE, :HD] = (
                                wide * row_scale(wide) * key_gain
                            ).astype(jnp.bfloat16)

            for h in range(count):
                x = xs[h]
                hidden = x * row_scale(x) * (1.0 + gain(h, 0)) + gain(h, 1)
                new_values = hidden.astype(jnp.bfloat16)
                scaled = hidden * row_scale(hidden)
                new_keys = (scaled * gain(h, 3)).astype(jnp.bfloat16)
                query_bufs[h][:, :HD] = (scaled * (gain(h, 2) * QUERY_SCALE)).astype(jnp.bfloat16)
                for column in range(WT):
                    at = column * COLKEYS + 6 * TILE
                    rows = slice(column * 2 * TILE, (column + 1) * 2 * TILE)
                    value_bufs[h][at : at + 2 * TILE, :HD] = new_values[rows]
                    key_bufs[h][at : at + 2 * TILE, :HD] = new_keys[rows]

            sums = [[] for _ in range(count)]
            for column in range(WT):
                keys = slice(column * COLKEYS, (column + 1) * COLKEYS)
                begin, end = QUERY_ROWS[column]
                for h in range(count):
                    scores = lax.dot_general(
                        query_bufs[h][begin:end],
                        key_bufs[h][keys],
                        (((1,), (1,)), ((), ())),
                        preferred_element_type=jnp.float32,
                    )
                    weights = jnp.exp2(scores).astype(jnp.bfloat16)
                    sums[h].append(
                        jnp.dot(weights, value_bufs[h][keys], preferred_element_type=jnp.float32)
                    )
            results = []
            for h in range(count):
                left, middle, right = sums[h]
                total = [
                    left[:128] + middle[:128],
                    left[128:] + middle[128:256] + right[:128],
                    middle[256:] + right[128:],
                ]
                mixed = jnp.concatenate([t[:, :HD] / t[:, HD:] for t in total], axis=0)
                out = (xs[h] + gain(h, 4) * mixed).astype(jnp.bfloat16)
                for i, (row, column) in enumerate(column_order()):
                    tile = (row * WT + column) * TILE
                    out_buf[h, layer, tile : tile + TILE] = out[i * TILE : (i + 1) * TILE]
                out_copy(layer, h).start()
                results.append(out.astype(jnp.float32))
            return tuple(results)

        last = lax.fori_loop(0, LAYERS, layer_step, tuple(first))
        ends = []
        for h in range(count):
            x_buf[h] = last[h].astype(jnp.bfloat16)
            ends.append(pltpu.make_async_copy(x_buf.at[h], x_out.at[h], x_sems.at[h]))
            ends[-1].start()
        for h in range(count):
            for layer in range(LAYERS):
                out_copy(layer, h).wait()
            ends[h].wait()

    works = upper == stage
    if heads[0][0] == 2:
        works = works & (lax.rem(mine, 2) == 0)
    pl.when(works)(lambda: work(n_heads))


def attention(place, x_in, params, bias, kv, heads, stage, previous, before, first_row, rows, cost):
    n_heads = len(heads)
    skipped = list(previous) + list(before)
    n_copies = max(len(head[1]) for head in heads)
    return pl.pallas_call(
        functools.partial(attention_kernel, (heads, stage, len(kv), len(skipped), first_row)),
        out_shape=[
            jax.ShapeDtypeStruct((LAYERS, rows, HD), jnp.bfloat16),
            jax.ShapeDtypeStruct((n_heads, ROWS, HD), jnp.bfloat16),
        ],
        in_specs=[SMEM, HBM if stage == 0 else ANY, VMEM, VMEM]
        + [ANY] * len(kv)
        + [HBM] * len(previous)
        + [ANY] * len(before),
        out_specs=[HBM, ANY],
        scratch_shapes=[
            pltpu.VMEM((n_heads, ROWS, HD), jnp.bfloat16),
            pltpu.VMEM((n_heads, LAYERS, 3, ROWS, HD), jnp.bfloat16),
            pltpu.VMEM((n_heads, LAYERS, ROWS, HD), jnp.bfloat16),
        ]
        + [pltpu.VMEM((KEYS, 2 * HD), jnp.bfloat16)] * (2 * n_heads)
        + [pltpu.VMEM((ROWS, 2 * HD), jnp.bfloat16)] * n_heads
        + [
            pltpu.SemaphoreType.DMA((n_heads, LAYERS, n_copies)),
            pltpu.SemaphoreType.DMA((n_heads,)),
            pltpu.SemaphoreType.DMA((n_heads, LAYERS)),
        ],
        input_output_aliases={4 + len(kv): 0} if previous else {},
        compiler_params=pltpu.CompilerParams(vmem_limit_bytes=32 * 1024 * 1024),
        cost_estimate=cost,
    )(place, x_in, params, bias, *kv, *skipped)


def bias_table(tile_list, tile_count, plan, block_index):
    slot_live = jnp.arange(tile_list.shape[1])[None, :] < tile_count[:, None]
    window_ids = (block_index - 1) * NPATCH + jnp.arange(3 * NPATCH)
    window = jnp.any(
        (tile_list[:, :, None] == window_ids[None, None, :]) & slot_live[:, :, None], axis=1
    )
    patches = jnp.arange(NPATCH)
    position = jnp.sum(jnp.where(plan[None, :] == patches[:, None], patches[None, :], 0), axis=1)
    is_new = position[None, :] <= position[:, None]
    near = window[:, NPATCH : 2 * NPATCH]
    kinds = [window[:, :NPATCH], window[:, 2 * NPATCH :], near & ~is_new, near & is_new]
    listed = jnp.stack(kinds, axis=1).reshape(NPATCH, 4, HT, WT).transpose(0, 3, 1, 2)
    listed = listed.reshape(HT, WT, 4 * NPATCH).transpose(1, 0, 2).reshape(NPATCH, 4 * NPATCH)
    bias = jnp.where(listed, 0.0, MASKED).astype(jnp.bfloat16)
    bias = jnp.pad(bias, ((0, 0), (0, HD - 4 * NPATCH)))
    return jnp.repeat(bias, TILE, axis=0)


def on_device(
    tokens_in,
    stale_values,
    mod_scale,
    mod_shift,
    query_gain,
    key_gain,
    branch_gain,
    tile_list,
    tile_count,
    patch_order,
):
    n_section, n_seq = lax.axis_size("section"), lax.axis_size("seq")
    section = lax.axis_index("section")
    mine = lax.rem(section, GROUP)
    upper = lax.div(section, GROUP)
    groups = [list(range(GROUP)), list(range(GROUP, 2 * GROUP))]
    forward = [(i, i + 1) for i in range(n_seq - 1)]
    backward = [(i + 1, i) for i in range(n_seq - 1)]
    place = jnp.stack([section, mine, upper]).astype(jnp.int32)

    def exchange(array):
        return lax.all_to_all(array, "section", 0, 0, axis_index_groups=groups, tiled=True)

    def both_ways(array):
        return lax.ppermute(array, "seq", forward), lax.ppermute(array, "seq", backward)

    def shape(*dims):
        return jax.ShapeDtypeStruct(dims, jnp.bfloat16)

    def call(kernel, out_shape, in_specs, out_specs, *args, **options):
        return pl.pallas_call(
            kernel,
            out_shape=out_shape,
            in_specs=in_specs,
            out_specs=out_specs,
            cost_estimate=SMALL,
            **options,
        )(*args)

    raw = call(
        eight_heads_kernel,
        shape(GROUP, ROWS, HD),
        [pl.BlockSpec((1, ROWS, GROUP * HD), lambda i: (0, 0, 0))],
        pl.BlockSpec((GROUP, ROWS, HD), lambda i: (0, 0, 0)),
        stale_values,
        grid=(1,),
    )
    raw_sides = both_ways(raw)
    own = exchange(
        call(
            by_owner_kernel,
            shape(GROUP, 2 * ROWS + HALF, HD),
            [VMEM, ANY],
            VMEM,
            stale_values,
            raw,
        )
    )

    vectors = jnp.concatenate(
        [mod_scale, mod_shift, query_gain, key_gain, branch_gain], axis=0
    ).reshape(5, 20, HD)
    vectors = jnp.concatenate(
        [
            vectors[:, :GROUP],
            vectors[:, GROUP : 2 * GROUP],
            jnp.repeat(vectors[:, 2 * GROUP :], 2, axis=1),
        ],
        axis=-1,
    ).transpose(1, 0, 2)
    vectors = call(
        pass_kernel,
        jax.ShapeDtypeStruct(vectors.shape, vectors.dtype),
        [HBM, ANY],
        HBM,
        vectors,
        own,
        input_output_aliases={0: 0},
    )
    params = exchange(vectors)
    bias = bias_table(tile_list, tile_count, patch_order[0], lax.axis_index("seq"))

    own_b, own_c = call(
        split_kernel,
        [shape(GROUP, ROWS, HD), shape(GROUP, HALF, HD)],
        [VMEM, ANY, ANY, ANY],
        [VMEM, VMEM],
        own,
        *raw_sides,
        params,
    )
    sides_b = both_ways(own_b)
    joined = call(
        join_kernel, shape(GROUP, 2 * ROWS, HD), [VMEM, VMEM, ANY], VMEM, *raw_sides, own_b
    )
    sides_a = exchange(joined)

    def to_first_core(array, step, from_core):
        pairs = []
        for s in range(from_core, n_section, 2):
            for f in range(n_seq):
                if 0 <= f + step < n_seq:
                    pairs.append((s * n_seq + f, (s - from_core) * n_seq + f + step))
        return lax.ppermute(array, ("section", "seq"), pairs)

    sides_c = [to_first_core(own_c, step, c) for step in (1, -1) for c in range(2)]
    own_c_other = to_first_core(own_c, 0, 1)

    head_a = (0, ((0, 0, ROWS, 0, 0), (1, 0, ROWS, 1, 0), (1, ROWS, ROWS, 2, 0)))
    head_b = (1, tuple((i, 0, ROWS, i, 0) for i in range(3)))
    head_c = (2, tuple((i, 0, HALF, i // 2, (i % 2) * HALF) for i in range(6)))
    kinds = {
        "a": ([own, sides_a], (head_a,), 0, ROWS),
        "b": ([own_b, *sides_b], (head_b,), 0, 2 * ROWS),
        "c": ([own_c, own_c_other, *sides_c], (head_c,), ROWS, 2 * ROWS),
    }

    def run(name, stage, x_in, previous, before, cost=SMALL):
        kv, heads, *rows = kinds[name]
        return attention(place, x_in, params, bias, kv, heads, stage, previous, before, *rows, cost)

    def hop(last, step):
        return lax.ppermute(last, "section", [(i, i + GROUP) for i in range(0, GROUP, step)])

    def home(pieces, parts, out):
        before = [] if out is None else [out]
        return call(
            functools.partial(home_kernel, parts),
            shape(1, ROWS, CHANNELS),
            [VMEM] * len(pieces) + [HBM] * len(before),
            HBM,
            *pieces,
            *before,
            scratch_shapes=[pltpu.SemaphoreType.DMA((3 * GROUP,))],
            input_output_aliases={len(pieces): 0} if before else {},
        )

    layers_a, last_a = run("a", 0, tokens_in, [], [])
    next_a = hop(last_a, 1)
    layers, last_b = run("b", 0, tokens_in, [], [last_a], LARGE)
    next_b = hop(last_b, 1)
    layers_a, done_a = run("a", 1, next_a, [layers_a], [last_b])
    arrived_a = exchange(layers_a)
    layers, last_c = run("c", 0, tokens_in, [layers], [done_a, next_b], LARGE)
    next_c = hop(last_c, 2)
    layers, done_b = run("b", 1, next_b, [layers], [], LARGE)
    layers, _ = run("c", 1, next_c, [layers], [arrived_a])
    out = home([arrived_a], ((0, 0, 0, 1),), None)
    out = home([exchange(layers)], ((0, 0, GROUP, 1), (0, ROWS, 2 * GROUP, 2)), out)
    return out


def solution(mesh):
    return jax.shard_map(
        on_device,
        mesh=mesh,
        in_specs=(
            P("seq", None),
            P("section", "seq", None),
            P("section", None),
            P("section", None),
            P("section", None),
            P("section", None),
            P("section", None),
            P("seq", None),
            P("seq"),
            P("seq", None),
        ),
        out_specs=P("section", "seq", None),
        check_vma=False,
    )
```
